32 devices in a mesh: groups: 2 (over x), seq: 16 (over z, y, core).
Axes of the slice: x: 2, y: 2, z: 4, core: 2. Of those that a mesh axis runs over, the one named last changes fastest.
Arguments:
- queries: bfloat16 [8192, 1024], P(('groups', 'seq')), parts along dimension 0, may hold values from -6 to 6
- keys: bfloat16 [8192, 1024], P(('groups', 'seq')), parts along dimension 0, may hold values from -6 to 6
- values: bfloat16 [8192, 1024], P(('groups', 'seq')), parts along dimension 0, may hold values from -6 to 6
- out_grad: bfloat16 [8192, 1024], P(('groups', 'seq')), parts along dimension 0, may hold values from -0.09375 to 0.09375
- maps: float32 [2, 8, 128, 128], replicated, may hold values from -0.5 to 0.5
- gain: bfloat16 [1024], replicated, may hold values from 0.25 to 1.75
- first_moment: float32 [2048, 128], P('seq'), may hold values from -1.8 to 1.8
- second_moment: float32 [2048, 128], P('seq'), may hold values from 0.01 to 0.3
Outputs:
- attention: bfloat16 [8192, 1024], P(('groups', 'seq')), parts along dimension 0
- new_maps: float32 [4, 8, 128, 128], P('groups'), parts along dimension 0
- new_moments: float32 [4, 2048, 128], P('groups', 'seq'), parts along dimension 0
The draws below stay inside these ranges and needn't reach their ends.
There are 2 independent parts, one for each index of `groups`. The reference program is written for one: setup_inputs(seed, part) draws one part's arguments, and reference() takes and returns one part's arrays. A program takes and returns all parts, laid end to end along the dimension named above; an argument that names none is the same for every part. Nothing has to cross between parts.
All inputs are finite; a program needn't handle non-finite values.
Results may differ from the reference program's by a relative error of at most 0.0057.
Values sent between devices are 32-bit elements; how exact they have to be, the bound alone decides.
A program may use at most 320 MiB of HBM per device.

```python
import math
import jax
import jax.numpy as jnp
from jax import lax

H = 8
E = 128
TOK_DEV = 256
SPAN = 256
OPT_STEP = 10
TOKENS = 4096
N_SEQ = 16


def block_levels(own_key, extent, cuts, least, top_value):
    factor_of, own = 1.0, jax.random.fold_in(own_key, 6)
    for dim, blocks in cuts:
        draws = jnp.exp(jax.random.uniform(jax.random.fold_in(own, dim), (blocks,), jnp.float32, least / len(cuts), top_value / len(cuts)))
        factor_of = factor_of * jnp.repeat(draws, extent[dim] // blocks).reshape([-1 if axis == dim else 1 for axis in range(len(extent))])
    return factor_of


def scatter_about(rng, shape, deviation, most, cuts=(), kind=jnp.bfloat16):
    result = deviation * jax.random.normal(rng, shape, jnp.float32)
    if cuts:
        result = result * block_levels(rng, shape, cuts, -0.22, 0.18)
    return jnp.clip(result, -most, most).astype(kind)


def setup_inputs(seed: int = 0, part: int = 0) -> dict:
    key_list = jax.random.split(jax.random.key(seed), 9)
    own_keys = jax.random.split(jax.random.fold_in(key_list[8], part), 9)
    queries = scatter_about(own_keys[0], (TOKENS, H * E), 1.0, 6.0, ((0, 16),))
    keys = scatter_about(own_keys[1], (TOKENS, H * E), 1.0, 6.0, ((0, 16),))
    values = scatter_about(own_keys[2], (TOKENS, H * E), 1.0, 6.0, ((0, 16),))
    out_grad = scatter_about(own_keys[3], (TOKENS, H * E), (1.0 / (TOK_DEV * N_SEQ) ** 0.5), 0.09375, ((0, 16),))
    maps = scatter_about(key_list[4], (2, H, E, E), E ** -0.5, 0.5, (), jnp.float32)
    gain = jnp.clip(1.0 + 0.15 * jax.random.normal(key_list[5], (H * E,), jnp.float32), 0.25, 1.75).astype(jnp.bfloat16)
    first_moment = scatter_about(key_list[6], (2 * H * E, E), 0.3, 1.8, ((0, 16),), jnp.float32)
    second_moment = jnp.clip(jnp.exp(math.log(0.3) - 3.4011974 * jax.random.uniform(key_list[7], (2 * H * E, E), jnp.float32) ** block_levels(key_list[7], (2 * H * E, E), ((0, 16),), -0.2, 0.2)), 0.01, 0.3)
    return dict(queries=queries, keys=keys, values=values, out_grad=out_grad, maps=maps, gain=gain, first_moment=first_moment, second_moment=second_moment)


BETA_ONE = 0.9
BETA_TWO = 0.95
RATE = 0.01
TINY = 1e-08
NORM_EPS = 1e-06

def widen(tensor):
    return tensor.astype(jnp.float32)

def causal(length):
    places = jnp.arange(length)
    return places[:, None] >= places[None, :]

def silu_slope(preact):
    sigmoid = jax.nn.sigmoid(preact)
    return sigmoid * (1.0 + preact * (1.0 - sigmoid))

def adam_rows(gradient, weights, first_old, second_old):
    first_new = BETA_ONE * first_old + (1.0 - BETA_ONE) * gradient
    second_new = BETA_TWO * second_old + (1.0 - BETA_TWO) * gradient * gradient
    first_hat = first_new / (1.0 - BETA_ONE ** OPT_STEP)
    second_hat = second_new / (1.0 - BETA_TWO ** OPT_STEP)
    return (weights - RATE * first_hat / (jnp.sqrt(second_hat) + TINY), first_new, second_new)

def head_pass(pieces):
    query_in, key_in, value_in, grad_in, map_pair, gain_head = pieces
    low_maps = map_pair.astype(jnp.bfloat16)
    pre_query = jnp.einsum('nche,hef->nchf', widen(query_in), widen(low_maps[0]))
    pre_key = jnp.einsum('nche,hef->nchf', widen(key_in), widen(low_maps[1]))
    feat_query = jax.nn.silu(pre_query).astype(jnp.bfloat16)
    feat_key = jax.nn.silu(pre_key).astype(jnp.bfloat16)
    own_states = jnp.einsum('ncht,ncho->nhto', widen(feat_key), widen(value_in))
    before = (jnp.cumsum(own_states, 0) - own_states).astype(jnp.bfloat16)
    masked = causal(SPAN)[None, None]
    inter = jnp.einsum('ncht,nhto->ncho', widen(feat_query), widen(before))
    scores = jnp.einsum('ncht,nsht->nhcs', widen(feat_query), widen(feat_key))
    scores = jnp.where(masked, scores, 0.0).astype(jnp.bfloat16)
    intra = jnp.einsum('nhcs,nsho->ncho', widen(scores), widen(value_in))
    raw = inter + intra
    scale = lax.rsqrt(lax.optimization_barrier(jnp.mean(raw * raw, -1, keepdims=True)) + NORM_EPS)
    unit = raw * scale
    gain_wide = widen(gain_head)
    output = (unit * gain_wide).astype(jnp.bfloat16)
    dunit = widen(grad_in) * gain_wide
    grad_raw = (scale * (dunit - unit * lax.optimization_barrier(jnp.mean(dunit * unit, -1, keepdims=True)))).astype(jnp.bfloat16)
    grad_states = jnp.einsum('ncht,ncho->nhto', widen(feat_query), widen(grad_raw))
    after = (lax.optimization_barrier(jnp.sum(grad_states, 0))[None] - jnp.cumsum(grad_states, 0)).astype(jnp.bfloat16)
    pscores = jnp.einsum('ncho,nsho->nhcs', widen(grad_raw), widen(value_in))
    pscores = jnp.where(masked, pscores, 0.0).astype(jnp.bfloat16)
    grad_fq = jnp.einsum('ncho,nhto->ncht', widen(grad_raw), widen(before))
    grad_fq = grad_fq + jnp.einsum('nhcs,nsht->ncht', widen(pscores), widen(feat_key))
    grad_fk = jnp.einsum('ncho,nhto->ncht', widen(value_in), widen(after))
    grad_fk = grad_fk + jnp.einsum('nhcs,ncht->nsht', widen(pscores), widen(feat_query))
    grad_pq = (grad_fq * silu_slope(pre_query)).astype(jnp.bfloat16)
    grad_pk = (grad_fk * silu_slope(pre_key)).astype(jnp.bfloat16)
    grad_query = jnp.einsum('ncht,nchu->htu', widen(query_in), widen(grad_pq))
    grad_key = jnp.einsum('ncht,nchu->htu', widen(key_in), widen(grad_pk))
    return (output, jnp.stack([grad_query, grad_key]))

def reference(queries, keys, values, out_grad, maps, gain, first_moment, second_moment):
    total = queries.shape[0]
    blocks = total // SPAN

    def arrange(tensor):
        return tensor.reshape(blocks, SPAN, H, E).transpose(2, 0, 1, 3)[:, :, :, None, :]
    pieces = (arrange(queries), arrange(keys), arrange(values), arrange(out_grad), maps.transpose(1, 0, 2, 3)[:, :, None], gain.reshape(H, 1, E))
    outputs, grads = lax.map(head_pass, pieces)
    attention = outputs[:, :, :, 0, :].transpose(1, 2, 0, 3).reshape(total, H * E)
    gradient = grads[:, :, 0].transpose(1, 0, 2, 3).reshape(2 * H * E, E)
    new_rows, first_new, second_new = adam_rows(gradient, maps.reshape(2 * H * E, E), first_moment, second_moment)
    return (attention, new_rows.reshape(2, H, E, E), jnp.stack([first_new, second_new]))
```

```python
import functools

import jax
import jax.numpy as jnp
from jax import lax
from jax.experimental import pallas as pl
from jax.experimental.pallas import tpu as pltpu
from jax.sharding import PartitionSpec as P

H = 8
E = 128
SPAN = 256
OPT_STEP = 10
CHUNKS = 2

BETA_ONE = 0.9
BETA_TWO = 0.95
RATE = 0.01
TINY = 1e-08
NORM_EPS = 1e-06

F32 = jnp.float32
BF16 = jnp.bfloat16


def dot(left, right, left_dim, right_dim):
    return lax.dot_general(
        left, right, (((left_dim,), (right_dim,)), ((), ())), preferred_element_type=F32
    )


def adam_rows(gradient, weights, first_old, second_old):
    first_new = BETA_ONE * first_old + (1.0 - BETA_ONE) * gradient
    second_new = BETA_TWO * second_old + (1.0 - BETA_TWO) * gradient * gradient
    first_hat = first_new / (1.0 - BETA_ONE**OPT_STEP)
    second_hat = second_new / (1.0 - BETA_TWO**OPT_STEP)
    return (weights - RATE * first_hat / (jnp.sqrt(second_hat) + TINY), first_new, second_new)


def layout(count):
    chips = count // 2
    row = 1
    while row * row * 4 <= chips:
        row *= 2
    plane = 2 * row
    return count // plane, plane


def kernel(
    depth, plane, share,
    queries, keys, values, out_grad, maps, gain, first_old, second_old,
    attention, new_maps, new_moments,
    feat_q, feat_k, slope_q, slope_k, raw_part, grad_raw, local_fk,
    states, plane_in, chain_in, chain_out, back, summed,
    grads, grads_in, grads_part, rows_in,
    send_a, recv_a, send_z, recv_z, send_c, recv_c,
    send_r, recv_r, send_rz, recv_rz, send_g, recv_g, send_p, recv_p,
):
    group = lax.axis_index("groups")
    me = lax.axis_index("seq")
    level = me // plane
    place = me % plane
    half = depth // 2
    rows = H * E // plane
    part = rows // CHUNKS
    peers = [(place + step) % plane for step in range(1, plane)]
    levels = [(level + step) % depth for step in range(1, depth)]

    def remote(src, dst, send, recv, to_level, to_place):
        return pltpu.make_async_remote_copy(
            src_ref=src, dst_ref=dst, send_sem=send, recv_sem=recv,
            device_id=(group, to_level * plane + to_place),
            device_id_type=pl.DeviceIdType.MESH,
        )

    def span(start, size):
        return pl.ds(pl.multiple_of(start, size), size)

    barrier = pltpu.get_barrier_semaphore()
    for peer in peers:
        pl.semaphore_signal(
            barrier, inc=1, device_id=(group, level * plane + peer),
            device_id_type=pl.DeviceIdType.MESH,
        )
    for other in levels:
        pl.semaphore_signal(
            barrier, inc=1, device_id=(group, other * plane + place),
            device_id_type=pl.DeviceIdType.MESH,
        )

    def heads(body):
        def pair(step, carry):
            body(2 * step)
            body(2 * step + 1)
            return carry

        lax.fori_loop(0, H // 2, pair, 0)

    def masked(scores):
        row = lax.broadcasted_iota(jnp.int32, (SPAN, SPAN), 0)
        column = lax.broadcasted_iota(jnp.int32, (SPAN, SPAN), 1)
        return jnp.where(row >= column, scores, 0.0).astype(BF16)

    def features(head):
        cols = span(head * E, E)

        def one(source, weights, feat, slope):
            pre = dot(source[:, cols], weights.astype(BF16), 1, 0)
            sigmoid = 1.0 / (1.0 + jnp.exp(-pre))
            feat[:, cols] = (pre * sigmoid).astype(BF16)
            slope[:, cols] = sigmoid * (1.0 + pre * (1.0 - sigmoid))

        one(keys, maps[span((H + head) * E, E), :], feat_k, slope_k)
        one(queries, maps[span(head * E, E), :], feat_q, slope_q)
        states[0, span(head * E, E), :] = dot(feat_k[:, cols], values[:, cols], 0, 0)

    heads(features)
    pl.semaphore_wait(barrier, plane + depth - 2)

    def chunk_copy(way, peer, chunk):
        return remote(
            states.at[way, span(peer * rows + chunk * part, part)],
            plane_in.at[way, place, pl.ds(chunk * part, part)],
            send_a.at[way, peer, chunk], recv_a.at[way, place, chunk], level, peer,
        )

    def chunk_arrival(way, peer, chunk):
        return remote(
            states.at[way, span(place * rows + chunk * part, part)],
            plane_in.at[way, peer, pl.ds(chunk * part, part)],
            send_a.at[way, place, chunk], recv_a.at[way, peer, chunk], level, peer,
        )

    def chain_copy(way, chunk):
        here = pl.ds(chunk * part, part)
        return remote(
            chain_out.at[way, here], chain_in.at[way, here],
            send_z.at[way, chunk], recv_z.at[way, chunk],
            (level + (depth - 1 if way else 1)) % depth, place,
        )

    def back_copy(way, peer, chunk):
        return remote(
            back.at[way, peer, pl.ds(chunk * part, part)],
            summed.at[way, span(place * rows + chunk * part, part)],
            send_c.at[way, peer, chunk], recv_c.at[way, place, chunk], level, peer,
        )

    def back_arrival(way, peer, chunk):
        return remote(
            back.at[way, place, pl.ds(chunk * part, part)],
            summed.at[way, span(peer * rows + chunk * part, part)],
            send_c.at[way, place, chunk], recv_c.at[way, peer, chunk], level, peer,
        )

    def scan_start(way):
        for chunk in range(CHUNKS):
            for peer in peers:
                chunk_copy(way, peer, chunk).start()
        plane_in[way, place] = states[way, span(place * rows, rows), :]

    def scan_middle(way):
        first, last = (depth - 1, 0) if way else (0, depth - 1)
        for chunk in range(CHUNKS):
            here = pl.ds(chunk * part, part)
            for peer in peers:
                chunk_arrival(way, peer, chunk).wait_recv()
            total = plane_in[way, 0, here, :]
            for member in range(1, plane):
                total = total + plane_in[way, member, here, :]

            @pl.when(level != first)
            def _():
                chain_copy(way, chunk).wait_recv()

            @pl.when(level == first)
            def _():
                chain_in[way, here, :] = jnp.zeros((part, E), F32)

            running = chain_in[way, here, :]

            @pl.when(level != last)
            def _():
                chain_out[way, here, :] = running + total
                chain_copy(way, chunk).start()

            members = range(plane)
            for member in reversed(members) if way else members:
                back[way, member, here, :] = running
                running = running + plane_in[way, member, here, :]
            for peer in peers:
                back_copy(way, peer, chunk).start()
            summed[way, span(place * rows + chunk * part, part), :] = back[way, place, here, :]

    def scan_end(way):
        for chunk in range(CHUNKS):
            for peer in peers:
                back_arrival(way, peer, chunk).wait_recv()

    def scan_drain(way):
        last = 0 if way else depth - 1
        for chunk in range(CHUNKS):
            for peer in peers:
                chunk_copy(way, peer, chunk).wait_send()
                back_copy(way, peer, chunk).wait_send()

            @pl.when(level != last)
            def _():
                chain_copy(way, chunk).wait_send()

    scan_start(0)

    def inside(head):
        cols = span(head * E, E)
        scores = masked(dot(feat_q[:, cols], feat_k[:, cols], 1, 1))
        raw_part[:, cols] = dot(scores, values[:, cols], 1, 0)

    heads(inside)
    scan_middle(0)
    scan_end(0)

    def forward(head):
        cols = span(head * E, E)
        before = summed[0, span(head * E, E), :].astype(BF16)
        raw = dot(feat_q[:, cols], before, 1, 0) + raw_part[:, cols]
        scale = lax.rsqrt(jnp.mean(raw * raw, -1, keepdims=True) + NORM_EPS)
        unit = raw * scale
        wide = gain[:, cols].astype(F32)
        attention[:, cols] = (unit * wide).astype(BF16)
        dunit = out_grad[:, cols].astype(F32) * wide
        inner = jnp.mean(dunit * unit, -1, keepdims=True)
        grad = (scale * (dunit - unit * inner)).astype(BF16)
        grad_raw[:, cols] = grad
        states[1, span(head * E, E), :] = dot(feat_q[:, cols], grad, 0, 0)

    heads(forward)
    scan_start(1)

    def grad_copy(side, which, peer):
        return remote(
            grads.at[side, span((which * plane + peer) * share, share)],
            grads_in.at[side, which, place],
            send_r.at[side, which, peer], recv_r.at[side, which, place], level, peer,
        )

    def grad_arrival(side, which, peer):
        return remote(
            grads.at[side, span((which * plane + place) * share, share)],
            grads_in.at[side, which, peer],
            send_r.at[side, which, place], recv_r.at[side, which, peer], level, peer,
        )

    def owner_copy(side, which):
        return remote(
            grads_part.at[side, which], rows_in.at[level],
            send_rz.at[side, which], recv_rz.at[level], side * half + which, place,
        )

    def owner_arrival(other):
        return remote(
            grads_part.at[0, 0], rows_in.at[other],
            send_rz.at[0, 0], recv_rz.at[other], other, place,
        )

    def map_rows(owner_level, owner_place):
        return new_maps.at[span((owner_level * plane + owner_place) * share, share)]

    def map_copy(side, other):
        return remote(
            map_rows(level, place), map_rows(level, place),
            send_g.at[other], recv_g.at[side, level - side * half], other, place,
        )

    def map_arrival(side, which):
        owner = side * half + which
        return remote(
            map_rows(owner, place), map_rows(owner, place),
            send_g.at[owner], recv_g.at[side, which], owner, place,
        )

    def spread_copy(side, which, peer):
        owner = side * half + which
        return remote(
            map_rows(owner, place), map_rows(owner, place),
            send_p.at[side, which, peer], recv_p.at[side, which, place], level, peer,
        )

    def spread_arrival(side, which, peer):
        owner = side * half + which
        return remote(
            map_rows(owner, peer), map_rows(owner, peer),
            send_p.at[side, which, place], recv_p.at[side, which, peer], level, peer,
        )

    def reduce_start(side):
        for which in range(half):
            for peer in peers:
                grad_copy(side, which, peer).start()

    def reduce_middle(side):
        for which in range(half):
            total = grads[side, span((which * plane + place) * share, share), :]
            for peer in peers:
                grad_arrival(side, which, peer).wait_recv()
                total = total + grads_in[side, which, peer]

            @pl.when(level == side * half + which)
            def _():
                rows_in[level] = total

            @pl.when(level != side * half + which)
            def _():
                grads_part[side, which] = total
                owner_copy(side, which).start()

    def update(side):
        @pl.when(level // half == side)
        def _():
            for other in levels:
                owner_arrival(other).wait_recv()
            gradient = rows_in[0]
            for other in range(1, depth):
                gradient = gradient + rows_in[other]
            mine = span(me * share, share)
            rows_new, first_new, second_new = adam_rows(
                gradient, maps[mine, :], first_old[...], second_old[...]
            )
            new_maps[mine, :] = rows_new
            new_moments[0] = first_new
            new_moments[1] = second_new
            for other in levels:
                map_copy(side, other).start()

    def spread(side):
        for which in range(half):

            @pl.when(level != side * half + which)
            def _():
                map_arrival(side, which).wait_recv()

            for peer in peers:
                spread_copy(side, which, peer).start()

    def spread_end(side):
        for which in range(half):
            for peer in peers:
                spread_arrival(side, which, peer).wait_recv()

    def drain(side):
        for which in range(half):
            for peer in peers:
                grad_copy(side, which, peer).wait_send()
                spread_copy(side, which, peer).wait_send()

            @pl.when(level != side * half + which)
            def _():
                owner_copy(side, which).wait_send()

        @pl.when(level // half == side)
        def _():
            for other in levels:
                map_copy(side, other).wait_send()

    def query_side(head):
        cols = span(head * E, E)
        grad = grad_raw[:, cols]
        pscores = masked(dot(grad, values[:, cols], 1, 1))
        before = summed[0, span(head * E, E), :].astype(BF16)
        grad_fq = dot(grad, before, 1, 1) + dot(pscores, feat_k[:, cols], 1, 0)
        local_fk[:, cols] = dot(pscores, feat_q[:, cols], 0, 0)
        grad_pq = (grad_fq * slope_q[:, cols]).astype(BF16)
        grads[0, span(head * E, E), :] = dot(queries[:, cols], grad_pq, 0, 0)

    heads(query_side)
    reduce_start(0)
    scan_middle(1)
    reduce_middle(0)
    scan_end(1)

    def key_side(head):
        cols = span(head * E, E)
        after = summed[1, span(head * E, E), :].astype(BF16)
        grad_fk = dot(values[:, cols], after, 1, 1) + local_fk[:, cols]
        grad_pk = (grad_fk * slope_k[:, cols]).astype(BF16)
        grads[1, span(head * E, E), :] = dot(keys[:, cols], grad_pk, 0, 0)

    heads(key_side)
    reduce_start(1)
    update(0)
    reduce_middle(1)
    spread(0)
    update(1)
    spread(1)
    spread_end(0)
    spread_end(1)
    scan_drain(0)
    scan_drain(1)
    drain(0)
    drain(1)


def local(count, queries, keys, values, out_grad, maps, gain, first_moment, second_moment):
    depth, plane = layout(count)
    half = depth // 2
    share = 2 * H * E // count
    rows = H * E // plane
    tokens = queries.shape[0]
    wide = (SPAN, H * E)
    dma = pltpu.SemaphoreType.DMA
    scratch = [
        pltpu.VMEM(wide, BF16),
        pltpu.VMEM(wide, BF16),
        pltpu.VMEM(wide, F32),
        pltpu.VMEM(wide, F32),
        pltpu.VMEM(wide, F32),
        pltpu.VMEM(wide, BF16),
        pltpu.VMEM(wide, F32),
        pltpu.VMEM((2, H * E, E), F32),
        pltpu.VMEM((2, plane, rows, E), F32),
        pltpu.VMEM((2, rows, E), F32),
        pltpu.VMEM((2, rows, E), F32),
        pltpu.VMEM((2, plane, rows, E), F32),
        pltpu.VMEM((2, H * E, E), F32),
        pltpu.VMEM((2, H * E, E), F32),
        pltpu.VMEM((2, half, plane, share, E), F32),
        pltpu.VMEM((2, half, share, E), F32),
        pltpu.VMEM((depth, share, E), F32),
        dma((2, plane, CHUNKS)),
        dma((2, plane, CHUNKS)),
        dma((2, CHUNKS)),
        dma((2, CHUNKS)),
        dma((2, plane, CHUNKS)),
        dma((2, plane, CHUNKS)),
        dma((2, half, plane)),
        dma((2, half, plane)),
        dma((2, half)),
        dma((depth,)),
        dma((depth,)),
        dma((2, half)),
        dma((2, half, plane)),
        dma((2, half, plane)),
    ]
    vmem = pl.BlockSpec(memory_space=pltpu.VMEM)
    attention, new_maps, new_moments = pl.pallas_call(
        functools.partial(kernel, depth, plane, share),
        out_shape=(
            jax.ShapeDtypeStruct((tokens, H * E), BF16),
            jax.ShapeDtypeStruct((2 * H * E, E), F32),
            jax.ShapeDtypeStruct((2, share, E), F32),
        ),
        in_specs=[vmem] * 8,
        out_specs=(vmem, vmem, vmem),
        scratch_shapes=scratch,
        compiler_params=pltpu.CompilerParams(
            collective_id=0, has_side_effects=True, vmem_limit_bytes=40 * 1024 * 1024
        ),
        name="layer",
    )(
        queries, keys, values, out_grad, maps.reshape(2 * H * E, E), gain.reshape(1, H * E),
        first_moment, second_moment,
    )
    return attention, new_maps.reshape(2, H, E, E), new_moments


def solution(mesh):
    in_specs = (
        P(("groups", "seq"), None),
        P(("groups", "seq"), None),
        P(("groups", "seq"), None),
        P(("groups", "seq"), None),
        P(),
        P(),
        P("seq", None),
        P("seq", None),
    )
    out_specs = (
        P(("groups", "seq"), None),
        P("groups", None, None, None),
        P("groups", "seq", None),
    )
    return jax.shard_map(
        functools.partial(local, mesh.shape["seq"]),
        mesh=mesh, in_specs=in_specs, out_specs=out_specs, check_vma=False,
    )
```

```python
import functools

import jax
import jax.numpy as jnp
from jax import lax
from jax.experimental import pallas as pl
from jax.experimental.pallas import tpu as pltpu
from jax.sharding import PartitionSpec as P

H = 8
E = 128
SPAN = 256
OPT_STEP = 10
PAIRS = 4

BETA_ONE = 0.9
BETA_TWO = 0.95
RATE = 0.01
TINY = 1e-08
NORM_EPS = 1e-06

F32 = jnp.float32
BF16 = jnp.bfloat16


def dot(left, right, left_dim, right_dim):
    return lax.dot_general(
        left, right, (((left_dim,), (right_dim,)), ((), ())), preferred_element_type=F32
    )


def adam_rows(gradient, weights, first_old, second_old):
    first_new = BETA_ONE * first_old + (1.0 - BETA_ONE) * gradient
    second_new = BETA_TWO * second_old + (1.0 - BETA_TWO) * gradient * gradient
    first_hat = first_new / (1.0 - BETA_ONE**OPT_STEP)
    second_hat = second_new / (1.0 - BETA_TWO**OPT_STEP)
    return (weights - RATE * first_hat / (jnp.sqrt(second_hat) + TINY), first_new, second_new)


def layout(count):
    chips = count // 2
    row = 1
    while row * row * 4 <= chips:
        row *= 2
    return chips // row, row


def kernel(
    depth, width, share,
    queries_hbm, keys_hbm, values_hbm, out_grad_hbm, maps_hbm, first_hbm, second_hbm, gain,
    attention, new_maps, new_moments,
    queries, keys, values, out_grad, maps, first_old, second_old,
    feat_q, feat_k, slope_q, slope_k, raw_part, grad_raw, local_fk,
    states, core_in, chip, row_in, chain_in, chain_out, share_out, summed,
    grads, grads_core, grads_chip, grads_row, grads_part, rows_in,
    load,
    send_core, recv_core, send_row, recv_row, send_z, recv_z, send_share, recv_share,
    send_rc, recv_rc, send_ry, recv_ry, send_rz, recv_rz,
    send_gz, recv_gz, send_gy, recv_gy, send_gc, recv_gc,
):
    group = lax.axis_index("groups")
    me = lax.axis_index("seq")
    plane = 2 * width
    level = me // plane
    row = (me // 2) % width
    core = me % 2
    other_core = 1 - core
    half = depth // 2
    chunks = half * width
    per_pair = chunks // PAIRS
    rows_beside = [(row + step) % width for step in range(1, width)]
    levels = [(level + step) % depth for step in range(1, depth)]

    def index(to_level, to_row, to_core):
        return to_level * plane + to_row * 2 + to_core

    def remote(src, dst, send, recv, to_level, to_row, to_core):
        return pltpu.make_async_remote_copy(
            src_ref=src, dst_ref=dst, send_sem=send, recv_sem=recv,
            device_id=(group, index(to_level, to_row, to_core)),
            device_id_type=pl.DeviceIdType.MESH,
        )

    def span(start, size):
        return pl.ds(pl.multiple_of(start, size), size)

    def head_rows(head):
        return span(head * E, E)

    def greet(to):
        pl.semaphore_signal(
            barrier, inc=1, device_id=(group, to), device_id_type=pl.DeviceIdType.MESH
        )

    loads = [
        pltpu.make_async_copy(src, dst, load.at[slot])
        for slot, (src, dst) in enumerate(
            (
                (keys_hbm, keys),
                (maps_hbm, maps),
                (values_hbm, values),
                (queries_hbm, queries),
                (out_grad_hbm, out_grad),
                (first_hbm, first_old),
                (second_hbm, second_old),
            )
        )
    ]
    for one in loads:
        one.start()

    barrier = pltpu.get_barrier_semaphore()
    greet(index(level, row, other_core))
    for beside in rows_beside:
        greet(index(level, beside, core))
    for other in levels:
        greet(index(other, row, core))

    def masked(scores):
        line = lax.broadcasted_iota(jnp.int32, (SPAN, SPAN), 0)
        column = lax.broadcasted_iota(jnp.int32, (SPAN, SPAN), 1)
        return jnp.where(line >= column, scores, 0.0).astype(BF16)

    def both(body, pair):
        body(2 * pair)
        body(2 * pair + 1)

    def core_copy(way, pair):
        return remote(
            states.at[way, head_rows(2 * pair + other_core)], core_in.at[way, pair],
            send_core.at[way, pair], recv_core.at[way, pair], level, row, other_core,
        )

    def row_copy(way, pair, beside):
        return remote(
            chip.at[way, pair], row_in.at[way, row, pair],
            send_row.at[way, beside, pair], recv_row.at[way, row, pair], level, beside, core,
        )

    def row_arrival(way, pair, beside):
        return remote(
            chip.at[way, pair], row_in.at[way, beside, pair],
            send_row.at[way, row, pair], recv_row.at[way, beside, pair], level, beside, core,
        )

    def chain_copy(way, pair):
        return remote(
            chain_out.at[way, pair], chain_in.at[way, pair],
            send_z.at[way, pair], recv_z.at[way, pair],
            (level + (depth - 1 if way else 1)) % depth, row, core,
        )

    def share_copy(way, pair):
        mine = head_rows(2 * pair + core)
        return remote(
            share_out.at[way, pair], summed.at[way, mine],
            send_share.at[way, pair], recv_share.at[way, pair], level, row, other_core,
        )

    def share_arrival(way, pair):
        theirs = head_rows(2 * pair + other_core)
        return remote(
            share_out.at[way, pair], summed.at[way, theirs],
            send_share.at[way, pair], recv_share.at[way, pair], level, row, other_core,
        )

    def scan_rows(way, pair):
        core_copy(way, pair).wait_recv()
        own = states[way, head_rows(2 * pair + core), :]
        total = own + core_in[way, pair]
        chip[way, pair] = total
        for beside in rows_beside:
            row_copy(way, pair, beside).start()
        row_in[way, row, pair] = total

    def scan_levels(way, pair, first):
        last = 0 if way else depth - 1

        def steps():
            for beside in rows_beside:
                row_arrival(way, pair, beside).wait_recv()
            ahead = jnp.zeros((E, E), F32)
            total = jnp.zeros((E, E), F32)
            for member in range(width):
                one = row_in[way, member, pair]
                total = total + one
                counts = (member > row) if way else (member < row)
                ahead = ahead + jnp.where(counts, one, 0.0)
            if first:
                chain_out[way, pair] = total
                chain_copy(way, pair).start()
            else:
                chain_copy(way, pair).wait_recv()
                running = chain_in[way, pair]
                ahead = ahead + running

                @pl.when(level != last)
                def _():
                    chain_out[way, pair] = running + total
                    chain_copy(way, pair).start()

            near = core == (1 if way else 0)
            mine = head_rows(2 * pair + core)
            share_out[way, pair] = ahead + jnp.where(near, states[way, mine, :], 0.0)
            share_copy(way, pair).start()
            summed[way, mine, :] = ahead + jnp.where(near, 0.0, core_in[way, pair])

        at_first = level == (depth - 1 if way else 0)
        pl.when(at_first if first else jnp.logical_not(at_first))(steps)

    def scan_drain(way):
        last = 0 if way else depth - 1
        for pair in range(PAIRS):
            core_copy(way, pair).wait_send()
            share_copy(way, pair).wait_send()
            for beside in rows_beside:
                row_copy(way, pair, beside).wait_send()

            @pl.when(level != last)
            def _():
                chain_copy(way, pair).wait_send()

    def piece(chunk, of_core):
        return span((chunk * 2 + of_core) * share, share)

    def reduce_core_copy(side, chunk):
        return remote(
            grads.at[side, piece(chunk, other_core)], grads_core.at[side, chunk],
            send_rc.at[side, chunk], recv_rc.at[side, chunk], level, row, other_core,
        )

    def reduce_row_copy(side, chunk):
        which, to_row = chunk // width, chunk % width
        return remote(
            grads_chip.at[side, chunk], grads_row.at[side, which, row],
            send_ry.at[side, chunk], recv_ry.at[side, which, row], level, to_row, core,
        )

    def reduce_row_arrival(side, which, beside):
        return remote(
            grads_chip.at[side, 0], grads_row.at[side, which, beside],
            send_ry.at[side, 0], recv_ry.at[side, which, beside], level, beside, core,
        )

    def owner_copy(side, which):
        return remote(
            grads_part.at[side, which], rows_in.at[level],
            send_rz.at[side, which], recv_rz.at[level], side * half + which, row, core,
        )

    def owner_arrival(other):
        return remote(
            grads_part.at[0, 0], rows_in.at[other],
            send_rz.at[0, 0], recv_rz.at[other], other, row, core,
        )

    def reduce_start(side, pair):
        for chunk in range(pair * per_pair, (pair + 1) * per_pair):
            reduce_core_copy(side, chunk).start()

    def reduce_rows(side, pair):
        for chunk in range(pair * per_pair, (pair + 1) * per_pair):
            which, to_row = chunk // width, chunk % width
            reduce_core_copy(side, chunk).wait_recv()
            total = grads[side, piece(chunk, core), :] + grads_core[side, chunk]

            @pl.when(row == to_row)
            def _():
                grads_row[side, which, row] = total

            @pl.when(row != to_row)
            def _():
                grads_chip[side, chunk] = total
                reduce_row_copy(side, chunk).start()

    def reduce_levels(side, which):
        for beside in rows_beside:
            reduce_row_arrival(side, which, beside).wait_recv()
        total = grads_row[side, which, 0]
        for member in range(1, width):
            total = total + grads_row[side, which, member]

        @pl.when(level == side * half + which)
        def _():
            rows_in[level] = total

        @pl.when(level != side * half + which)
        def _():
            grads_part[side, which] = total
            owner_copy(side, which).start()

    def map_rows(of_level, of_row, of_core):
        return new_maps.at[span(index(of_level, of_row, of_core) * share, share)]

    def map_level_copy(side, other):
        mine = map_rows(level, row, core)
        return remote(
            mine, mine, send_gz.at[other], recv_gz.at[side, level - side * half],
            other, row, core,
        )

    def map_level_arrival(side, which):
        owner = side * half + which
        theirs = map_rows(owner, row, core)
        return remote(
            theirs, theirs, send_gz.at[owner], recv_gz.at[side, which], owner, row, core
        )

    def map_row_copy(side, which, beside):
        mine = map_rows(side * half + which, row, core)
        return remote(
            mine, mine, send_gy.at[side, which, beside], recv_gy.at[side, which, row],
            level, beside, core,
        )

    def map_row_arrival(side, which, beside):
        theirs = map_rows(side * half + which, beside, core)
        return remote(
            theirs, theirs, send_gy.at[side, which, row], recv_gy.at[side, which, beside],
            level, beside, core,
        )

    def map_core_copy(side, which, of_row):
        mine = map_rows(side * half + which, of_row, core)
        return remote(
            mine, mine, send_gc.at[side, which, of_row], recv_gc.at[side, which, of_row],
            level, row, other_core,
        )

    def map_core_arrival(side, which, of_row):
        theirs = map_rows(side * half + which, of_row, other_core)
        return remote(
            theirs, theirs, send_gc.at[side, which, of_row], recv_gc.at[side, which, of_row],
            level, row, other_core,
        )

    def update(side):
        @pl.when(level // half == side)
        def _():
            for other in levels:
                owner_arrival(other).wait_recv()
            gradient = rows_in[0]
            for other in range(1, depth):
                gradient = gradient + rows_in[other]
            mine = span(me * share, share)
            rows_new, first_new, second_new = adam_rows(
                gradient, maps[mine, :], first_old[...], second_old[...]
            )
            new_maps[mine, :] = rows_new
            for other in levels:
                map_level_copy(side, other).start()
            new_moments[0] = first_new
            new_moments[1] = second_new

    def spread(side):
        for which in range(half):

            @pl.when(level != side * half + which)
            def _():
                map_level_arrival(side, which).wait_recv()

            for beside in rows_beside:
                map_row_copy(side, which, beside).start()
            map_core_copy(side, which, row).start()

    def spread_core(side):
        for which in range(half):
            for beside in rows_beside:
                map_row_arrival(side, which, beside).wait_recv()
                map_core_copy(side, which, beside).start()

    def spread_end(side):
        for which in range(half):
            for of_row in range(width):
                map_core_arrival(side, which, of_row).wait_recv()

    def drain(side):
        for chunk in range(chunks):
            reduce_core_copy(side, chunk).wait_send()

            @pl.when(row != chunk % width)
            def _():
                reduce_row_copy(side, chunk).wait_send()

        for which in range(half):
            for beside in rows_beside:
                map_row_copy(side, which, beside).wait_send()
            for of_row in range(width):
                map_core_copy(side, which, of_row).wait_send()

            @pl.when(level != side * half + which)
            def _():
                owner_copy(side, which).wait_send()

        @pl.when(level // half == side)
        def _():
            for other in levels:
                map_level_copy(side, other).wait_send()

    def feature(source, weights, feat, slope, cols):
        pre = dot(source[:, cols], weights.astype(BF16), 1, 0)
        sigmoid = 1.0 / (1.0 + jnp.exp(-pre))
        feat[:, cols] = (pre * sigmoid).astype(BF16)
        slope[:, cols] = sigmoid * (1.0 + pre * (1.0 - sigmoid))

    def key_features(head):
        cols = head_rows(head)
        feature(keys, maps[head_rows(H + head), :], feat_k, slope_k, cols)
        states[0, head_rows(head), :] = dot(feat_k[:, cols], values[:, cols], 0, 0)

    def query_features(head):
        cols = head_rows(head)
        feature(queries, maps[head_rows(head), :], feat_q, slope_q, cols)

    def inside(head):
        cols = head_rows(head)
        scores = masked(dot(feat_q[:, cols], feat_k[:, cols], 1, 1))
        raw_part[:, cols] = dot(scores, values[:, cols], 1, 0)

    def forward(head):
        cols = head_rows(head)
        before = summed[0, head_rows(head), :].astype(BF16)
        raw = dot(feat_q[:, cols], before, 1, 0) + raw_part[:, cols]
        scale = lax.rsqrt(jnp.mean(raw * raw, -1, keepdims=True) + NORM_EPS)
        unit = raw * scale
        wide = gain[:, cols].astype(F32)
        attention[:, cols] = (unit * wide).astype(BF16)
        dunit = out_grad[:, cols].astype(F32) * wide
        inner = jnp.mean(dunit * unit, -1, keepdims=True)
        grad = (scale * (dunit - unit * inner)).astype(BF16)
        grad_raw[:, cols] = grad
        states[1, head_rows(head), :] = dot(feat_q[:, cols], grad, 0, 0)

    def query_side(head):
        cols = head_rows(head)
        grad = grad_raw[:, cols]
        pscores = masked(dot(grad, values[:, cols], 1, 1))
        before = summed[0, head_rows(head), :].astype(BF16)
        grad_fq = dot(grad, before, 1, 1) + dot(pscores, feat_k[:, cols], 1, 0)
        local_fk[:, cols] = dot(pscores, feat_q[:, cols], 0, 0)
        grad_pq = (grad_fq * slope_q[:, cols]).astype(BF16)
        grads[0, head_rows(head), :] = dot(queries[:, cols], grad_pq, 0, 0)

    def key_side(head):
        cols = head_rows(head)
        after = summed[1, head_rows(head), :].astype(BF16)
        grad_fk = dot(values[:, cols], after, 1, 1) + local_fk[:, cols]
        grad_pk = (grad_fk * slope_k[:, cols]).astype(BF16)
        grads[1, head_rows(head), :] = dot(keys[:, cols], grad_pk, 0, 0)

    def keys_pair(pair):
        both(key_features, pair)
        if pair == 0:
            pl.semaphore_wait(barrier, 1 + width - 1 + depth - 1)
        core_copy(0, pair).start()

    def forward_pair(pair):
        share_arrival(0, pair).wait_recv()
        both(forward, pair)
        core_copy(1, pair).start()

    def query_pair(pair):
        both(query_side, pair)
        reduce_start(0, pair)

    def key_pair(pair):
        share_arrival(1, pair).wait_recv()
        both(key_side, pair)
        reduce_start(1, pair)

    for one in loads[:3]:
        one.wait()
    keys_pair(0)
    keys_pair(1)
    scan_rows(0, 0)
    keys_pair(2)
    scan_rows(0, 1)
    keys_pair(3)
    scan_rows(0, 2)
    for one in loads[3:]:
        one.wait()
    both(query_features, 0)
    scan_rows(0, 3)
    both(query_features, 1)
    scan_levels(0, 0, True)
    both(query_features, 2)
    scan_levels(0, 1, True)
    both(query_features, 3)
    scan_levels(0, 2, True)
    both(inside, 0)
    scan_levels(0, 3, True)
    both(inside, 1)
    scan_levels(0, 0, False)
    both(inside, 2)
    scan_levels(0, 1, False)
    both(inside, 3)
    scan_levels(0, 2, False)
    forward_pair(0)
    scan_levels(0, 3, False)
    forward_pair(1)
    scan_rows(1, 0)
    forward_pair(2)
    scan_rows(1, 1)
    forward_pair(3)
    scan_rows(1, 2)
    query_pair(0)
    scan_rows(1, 3)
    scan_levels(1, 0, True)
    query_pair(1)
    scan_levels(1, 1, True)
    query_pair(2)
    scan_levels(1, 2, True)
    query_pair(3)
    scan_levels(1, 3, True)
    for pair in range(PAIRS):
        reduce_rows(0, pair)
    scan_levels(1, 0, False)
    scan_levels(1, 1, False)
    for which in range(half):
        reduce_levels(0, which)
    scan_levels(1, 2, False)
    key_pair(0)
    scan_levels(1, 3, False)
    key_pair(1)
    reduce_rows(1, 0)
    key_pair(2)
    reduce_rows(1, 1)
    key_pair(3)
    reduce_rows(1, 2)
    reduce_rows(1, 3)
    update(0)
    for which in range(half):
        reduce_levels(1, which)
    spread(0)
    update(1)
    spread_core(0)
    spread(1)
    spread_core(1)
    spread_end(0)
    spread_end(1)
    scan_drain(0)
    scan_drain(1)
    drain(0)
    drain(1)


def local(count, queries, keys, values, out_grad, maps, gain, first_moment, second_moment):
    depth, width = layout(count)
    half = depth // 2
    share = 2 * H * E // count
    tokens = queries.shape[0]
    wide = (SPAN, H * E)
    flat = (2 * H * E, E)
    square = (2, PAIRS, E, E)
    dma = pltpu.SemaphoreType.DMA
    chunks = half * width
    scratch = [
        pltpu.VMEM(wide, BF16),
        pltpu.VMEM(wide, BF16),
        pltpu.VMEM(wide, BF16),
        pltpu.VMEM(wide, BF16),
        pltpu.VMEM(flat, F32),
        pltpu.VMEM((share, E), F32),
        pltpu.VMEM((share, E), F32),
        pltpu.VMEM(wide, BF16),
        pltpu.VMEM(wide, BF16),
        pltpu.VMEM(wide, F32),
        pltpu.VMEM(wide, F32),
        pltpu.VMEM(wide, F32),
        pltpu.VMEM(wide, BF16),
        pltpu.VMEM(wide, F32),
        pltpu.VMEM((2, H * E, E), F32),
        pltpu.VMEM(square, F32),
        pltpu.VMEM(square, F32),
        pltpu.VMEM((2, width, PAIRS, E, E), F32),
        pltpu.VMEM(square, F32),
        pltpu.VMEM(square, F32),
        pltpu.VMEM(square, F32),
        pltpu.VMEM((2, H * E, E), F32),
        pltpu.VMEM((2, H * E, E), F32),
        pltpu.VMEM((2, chunks, share, E), F32),
        pltpu.VMEM((2, chunks, share, E), F32),
        pltpu.VMEM((2, half, width, share, E), F32),
        pltpu.VMEM((2, half, share, E), F32),
        pltpu.VMEM((depth, share, E), F32),
        dma((7,)),
        dma((2, PAIRS)),
        dma((2, PAIRS)),
        dma((2, width, PAIRS)),
        dma((2, width, PAIRS)),
        dma((2, PAIRS)),
        dma((2, PAIRS)),
        dma((2, PAIRS)),
        dma((2, PAIRS)),
        dma((2, chunks)),
        dma((2, chunks)),
        dma((2, chunks)),
        dma((2, half, width)),
        dma((2, half)),
        dma((depth,)),
        dma((depth,)),
        dma((2, half)),
        dma((2, half, width)),
        dma((2, half, width)),
        dma((2, half, width)),
        dma((2, half, width)),
    ]
    vmem = pl.BlockSpec(memory_space=pltpu.VMEM)
    anywhere = pl.BlockSpec(memory_space=pl.ANY)
    attention, new_maps, new_moments = pl.pallas_call(
        functools.partial(kernel, depth, width, share),
        out_shape=(
            jax.ShapeDtypeStruct((tokens, H * E), BF16),
            jax.ShapeDtypeStruct(flat, F32),
            jax.ShapeDtypeStruct((2, share, E), F32),
        ),
        in_specs=[anywhere] * 7 + [vmem],
        out_specs=(vmem, vmem, vmem),
        scratch_shapes=scratch,
        compiler_params=pltpu.CompilerParams(
            collective_id=0, has_side_effects=True, vmem_limit_bytes=60 * 1024 * 1024
        ),
        name="layer",
    )(
        queries, keys, values, out_grad, maps.reshape(flat),
        first_moment, second_moment, gain.reshape(1, H * E),
    )
    return attention, new_maps.reshape(2, H, E, E), new_moments


def solution(mesh):
    in_specs = (
        P(("groups", "seq"), None),
        P(("groups", "seq"), None),
        P(("groups", "seq"), None),
        P(("groups", "seq"), None),
        P(),
        P(),
        P("seq", None),
        P("seq", None),
    )
    out_specs = (
        P(("groups", "seq"), None),
        P("groups", None, None, None),
        P("groups", "seq", None),
    )
    return jax.shard_map(
        functools.partial(local, mesh.shape["seq"]),
        mesh=mesh, in_specs=in_specs, out_specs=out_specs, check_vma=False,
    )
```

```python
import functools

import jax
import jax.numpy as jnp
from jax import lax
from jax.experimental import pallas as pl
from jax.experimental.pallas import tpu as pltpu
from jax.sharding import PartitionSpec as P

H = 8
E = 128
SPAN = 256
OPT_STEP = 10
PAIRS = 4

BETA_ONE = 0.9
BETA_TWO = 0.95
RATE = 0.01
TINY = 1e-08
NORM_EPS = 1e-06

F32 = jnp.float32
BF16 = jnp.bfloat16


def dot(left, right, left_dim, right_dim):
    return lax.dot_general(
        left, right, (((left_dim,), (right_dim,)), ((), ())), preferred_element_type=F32
    )


def adam_rows(gradient, weights, first_old, second_old):
    first_new = BETA_ONE * first_old + (1.0 - BETA_ONE) * gradient
    second_new = BETA_TWO * second_old + (1.0 - BETA_TWO) * gradient * gradient
    first_hat = first_new / (1.0 - BETA_ONE**OPT_STEP)
    second_hat = second_new / (1.0 - BETA_TWO**OPT_STEP)
    return (weights - RATE * first_hat / (jnp.sqrt(second_hat) + TINY), first_new, second_new)


def layout(count):
    chips = count // 2
    row = 1
    while row * row * 4 <= chips:
        row *= 2
    return chips // row, row


def kernel(
    depth, width, share,
    queries_hbm, keys_hbm, values_hbm, out_grad_hbm, maps_hbm, first_hbm, second_hbm, gain,
    attention_hbm, new_maps, new_moments,
    queries, keys, values, out_grad, maps, first_old, second_old,
    gain_row, attention, turned_q, turned_k, turned_fq,
    feat_q, feat_k, slope_q, slope_k, raw_part, grad_raw, local_fk,
    states, core_in, chip, row_in, chain_in, chain_out, share_out, summed,
    grads, grads_core, grads_chip, grads_row, grads_part, rows_in,
    load, store,
    send_core, recv_core, send_row, recv_row, send_z, recv_z, send_share, recv_share,
    send_rc, recv_rc, send_ry, recv_ry, send_rz, recv_rz,
    send_gz, recv_gz, send_gy, recv_gy, send_gc, recv_gc,
):
    group = lax.axis_index("groups")
    me = lax.axis_index("seq")
    plane = 2 * width
    level = me // plane
    row = (me // 2) % width
    core = me % 2
    other_core = 1 - core
    half = depth // 2
    chunks = half * width
    per_pair = chunks // PAIRS
    rows_beside = [(row + step) % width for step in range(1, width)]
    levels = [(level + step) % depth for step in range(1, depth)]

    def index(to_level, to_row, to_core):
        return to_level * plane + to_row * 2 + to_core

    def remote(src, dst, send, recv, to_level, to_row, to_core):
        return pltpu.make_async_remote_copy(
            src_ref=src, dst_ref=dst, send_sem=send, recv_sem=recv,
            device_id=(group, index(to_level, to_row, to_core)),
            device_id_type=pl.DeviceIdType.MESH,
        )

    def span(start, size):
        return pl.ds(pl.multiple_of(start, size), size)

    def head_rows(head):
        return span(head * E, E)

    def greet(to):
        pl.semaphore_signal(
            barrier, inc=1, device_id=(group, to), device_id_type=pl.DeviceIdType.MESH
        )

    loads = [
        pltpu.make_async_copy(src, dst, load.at[slot])
        for slot, (src, dst) in enumerate(
            (
                (keys_hbm, keys),
                (maps_hbm, maps),
                (values_hbm, values),
                (queries_hbm, queries),
                (out_grad_hbm, out_grad),
                (first_hbm, first_old),
                (second_hbm, second_old),
            )
        )
    ]
    for one in loads:
        one.start()

    barrier = pltpu.get_barrier_semaphore()
    greet(index(level, row, other_core))
    for beside in rows_beside:
        greet(index(level, beside, core))
    for other in levels:
        greet(index(other, row, core))

    def masked(scores, turned=False):
        line = lax.broadcasted_iota(jnp.int32, (SPAN, SPAN), 0)
        column = lax.broadcasted_iota(jnp.int32, (SPAN, SPAN), 1)
        kept = (line <= column) if turned else (line >= column)
        return jnp.where(kept, scores, 0.0).astype(BF16)

    def both(body, pair):
        body(2 * pair)
        body(2 * pair + 1)

    def core_copy(way, pair):
        return remote(
            states.at[way, head_rows(2 * pair + other_core)], core_in.at[way, pair],
            send_core.at[way, pair], recv_core.at[way, pair], level, row, other_core,
        )

    def row_copy(way, pair, beside):
        return remote(
            chip.at[way, pair], row_in.at[way, row, pair],
            send_row.at[way, beside, pair], recv_row.at[way, row, pair], level, beside, core,
        )

    def row_arrival(way, pair, beside):
        return remote(
            chip.at[way, pair], row_in.at[way, beside, pair],
            send_row.at[way, row, pair], recv_row.at[way, beside, pair], level, beside, core,
        )

    def chain_copy(way, pair):
        return remote(
            chain_out.at[way, pair], chain_in.at[way, pair],
            send_z.at[way, pair], recv_z.at[way, pair],
            (level + (depth - 1 if way else 1)) % depth, row, core,
        )

    def share_copy(way, pair):
        mine = head_rows(2 * pair + core)
        return remote(
            share_out.at[way, pair], summed.at[way, mine],
            send_share.at[way, pair], recv_share.at[way, pair], level, row, other_core,
        )

    def share_arrival(way, pair):
        theirs = head_rows(2 * pair + other_core)
        return remote(
            share_out.at[way, pair], summed.at[way, theirs],
            send_share.at[way, pair], recv_share.at[way, pair], level, row, other_core,
        )

    def scan_rows(way, pair):
        core_copy(way, pair).wait_recv()
        own = states[way, head_rows(2 * pair + core), :]
        total = own + core_in[way, pair]
        chip[way, pair] = total
        for beside in rows_beside:
            row_copy(way, pair, beside).start()
        row_in[way, row, pair] = total

    def scan_levels(way, pair, first):
        last = 0 if way else depth - 1

        def steps():
            for beside in rows_beside:
                row_arrival(way, pair, beside).wait_recv()
            ahead = jnp.zeros((E, E), F32)
            total = jnp.zeros((E, E), F32)
            for member in range(width):
                one = row_in[way, member, pair]
                total = total + one
                counts = (member > row) if way else (member < row)
                ahead = ahead + jnp.where(counts, one, 0.0)
            if first:
                chain_out[way, pair] = total
                chain_copy(way, pair).start()
            else:
                chain_copy(way, pair).wait_recv()
                running = chain_in[way, pair]
                ahead = ahead + running

                @pl.when(level != last)
                def _():
                    chain_out[way, pair] = running + total
                    chain_copy(way, pair).start()

            near = core == (1 if way else 0)
            mine = head_rows(2 * pair + core)
            share_out[way, pair] = ahead + jnp.where(near, states[way, mine, :], 0.0)
            share_copy(way, pair).start()
            summed[way, mine, :] = ahead + jnp.where(near, 0.0, core_in[way, pair])

        at_first = level == (depth - 1 if way else 0)
        pl.when(at_first if first else jnp.logical_not(at_first))(steps)

    def scan_drain(way):
        last = 0 if way else depth - 1
        for pair in range(PAIRS):
            core_copy(way, pair).wait_send()
            share_copy(way, pair).wait_send()
            for beside in rows_beside:
                row_copy(way, pair, beside).wait_send()

            @pl.when(level != last)
            def _():
                chain_copy(way, pair).wait_send()

    def piece(chunk, of_core):
        return span((chunk * 2 + of_core) * share, share)

    def reduce_core_copy(side, chunk):
        return remote(
            grads.at[side, piece(chunk, other_core)], grads_core.at[side, chunk],
            send_rc.at[side, chunk], recv_rc.at[side, chunk], level, row, other_core,
        )

    def reduce_row_copy(side, chunk):
        which, to_row = chunk // width, chunk % width
        return remote(
            grads_chip.at[side, chunk], grads_row.at[side, which, row],
            send_ry.at[side, chunk], recv_ry.at[side, which, row], level, to_row, core,
        )

    def reduce_row_arrival(side, which, beside):
        return remote(
            grads_chip.at[side, 0], grads_row.at[side, which, beside],
            send_ry.at[side, 0], recv_ry.at[side, which, beside], level, beside, core,
        )

    def owner_copy(side, which):
        return remote(
            grads_part.at[side, which], rows_in.at[level],
            send_rz.at[side, which], recv_rz.at[level], side * half + which, row, core,
        )

    def owner_arrival(other):
        return remote(
            grads_part.at[0, 0], rows_in.at[other],
            send_rz.at[0, 0], recv_rz.at[other], other, row, core,
        )

    def reduce_start(side, pair):
        for chunk in range(pair * per_pair, (pair + 1) * per_pair):
            reduce_core_copy(side, chunk).start()

    def reduce_rows(side, pair):
        for chunk in range(pair * per_pair, (pair + 1) * per_pair):
            which, to_row = chunk // width, chunk % width
            reduce_core_copy(side, chunk).wait_recv()
            total = grads[side, piece(chunk, core), :] + grads_core[side, chunk]

            @pl.when(row == to_row)
            def _():
                grads_row[side, which, row] = total

            @pl.when(row != to_row)
            def _():
                grads_chip[side, chunk] = total
                reduce_row_copy(side, chunk).start()

    def reduce_levels(side, which):
        for beside in rows_beside:
            reduce_row_arrival(side, which, beside).wait_recv()
        total = grads_row[side, which, 0]
        for member in range(1, width):
            total = total + grads_row[side, which, member]

        @pl.when(level == side * half + which)
        def _():
            rows_in[level] = total

        @pl.when(level != side * half + which)
        def _():
            grads_part[side, which] = total
            owner_copy(side, which).start()

    def map_rows(of_level, of_row, of_core):
        return new_maps.at[span(index(of_level, of_row, of_core) * share, share)]

    def map_level_copy(side, other):
        mine = map_rows(level, row, core)
        return remote(
            mine, mine, send_gz.at[other], recv_gz.at[side, level - side * half],
            other, row, core,
        )

    def map_level_arrival(side, which):
        owner = side * half + which
        theirs = map_rows(owner, row, core)
        return remote(
            theirs, theirs, send_gz.at[owner], recv_gz.at[side, which], owner, row, core
        )

    def map_row_copy(side, which, beside):
        mine = map_rows(side * half + which, row, core)
        return remote(
            mine, mine, send_gy.at[side, which, beside], recv_gy.at[side, which, row],
            level, beside, core,
        )

    def map_row_arrival(side, which, beside):
        theirs = map_rows(side * half + which, beside, core)
        return remote(
            theirs, theirs, send_gy.at[side, which, row], recv_gy.at[side, which, beside],
            level, beside, core,
        )

    def map_core_copy(side, which, of_row):
        mine = map_rows(side * half + which, of_row, core)
        return remote(
            mine, mine, send_gc.at[side, which, of_row], recv_gc.at[side, which, of_row],
            level, row, other_core,
        )

    def map_core_arrival(side, which, of_row):
        theirs = map_rows(side * half + which, of_row, other_core)
        return remote(
            theirs, theirs, send_gc.at[side, which, of_row], recv_gc.at[side, which, of_row],
            level, row, other_core,
        )

    def update(side):
        @pl.when(level // half == side)
        def _():
            for other in levels:
                owner_arrival(other).wait_recv()
            gradient = rows_in[0]
            for other in range(1, depth):
                gradient = gradient + rows_in[other]
            mine = span(me * share, share)
            rows_new, first_new, second_new = adam_rows(
                gradient, maps[mine, :], first_old[...], second_old[...]
            )
            new_maps[mine, :] = rows_new
            for other in levels:
                map_level_copy(side, other).start()
            new_moments[0] = first_new
            new_moments[1] = second_new

    def spread(side):
        for which in range(half):

            @pl.when(level != side * half + which)
            def _():
                map_level_arrival(side, which).wait_recv()

            for beside in rows_beside:
                map_row_copy(side, which, beside).start()
            map_core_copy(side, which, row).start()

    def spread_core(side):
        for which in range(half):
            for beside in rows_beside:
                map_row_arrival(side, which, beside).wait_recv()
                map_core_copy(side, which, beside).start()

    def spread_end(side):
        for which in range(half):
            for of_row in range(width):
                map_core_arrival(side, which, of_row).wait_recv()

    def drain(side):
        for chunk in range(chunks):
            reduce_core_copy(side, chunk).wait_send()

            @pl.when(row != chunk % width)
            def _():
                reduce_row_copy(side, chunk).wait_send()

        for which in range(half):
            for beside in rows_beside:
                map_row_copy(side, which, beside).wait_send()
            for of_row in range(width):
                map_core_copy(side, which, of_row).wait_send()

            @pl.when(level != side * half + which)
            def _():
                owner_copy(side, which).wait_send()

        @pl.when(level // half == side)
        def _():
            for other in levels:
                map_level_copy(side, other).wait_send()

    def feature(source, weights, feat, slope, cols):
        pre = dot(source[:, cols], weights.astype(BF16), 1, 0)
        sigmoid = 1.0 / (1.0 + jnp.exp(-pre))
        feat[:, cols] = (pre * sigmoid).astype(BF16)
        slope[:, cols] = sigmoid * (1.0 + pre * (1.0 - sigmoid))

    def key_features(head):
        cols = head_rows(head)
        feature(keys, maps[head_rows(H + head), :], feat_k, slope_k, cols)
        states[0, head_rows(head), :] = dot(feat_k[:, cols], values[:, cols], 0, 0)

    def query_features(head):
        cols = head_rows(head)
        feature(queries, maps[head_rows(head), :], feat_q, slope_q, cols)
        turned_fq[head_rows(head), :] = feat_q[:, cols].T

    def inside(head):
        cols = head_rows(head)
        scores = masked(dot(feat_q[:, cols], feat_k[:, cols], 1, 1))
        raw_part[:, cols] = dot(scores, values[:, cols], 1, 0)
        turned_q[head_rows(head), :] = queries[:, cols].T
        turned_k[head_rows(head), :] = keys[:, cols].T

    def forward(head):
        cols = head_rows(head)
        before = summed[0, head_rows(head), :].astype(BF16)
        raw = dot(feat_q[:, cols], before, 1, 0) + raw_part[:, cols]
        scale = lax.rsqrt(jnp.mean(raw * raw, -1, keepdims=True) + NORM_EPS)
        unit = raw * scale
        wide = gain_row[:, cols]
        attention[:, cols] = (unit * wide).astype(BF16)
        dunit = out_grad[:, cols].astype(F32) * wide
        inner = jnp.mean(dunit * unit, -1, keepdims=True)
        grad = (scale * (dunit - unit * inner)).astype(BF16)
        grad_raw[:, cols] = grad
        states[1, head_rows(head), :] = dot(turned_fq[head_rows(head), :], grad, 1, 0)

    def query_side(head):
        cols = head_rows(head)
        grad = grad_raw[:, cols]
        pscores = masked(dot(grad, values[:, cols], 1, 1))
        before = summed[0, head_rows(head), :].astype(BF16)
        grad_fq = dot(grad, before, 1, 1) + dot(pscores, feat_k[:, cols], 1, 0)
        turned = masked(dot(values[:, cols], grad, 1, 1), True)
        local_fk[:, cols] = dot(turned, feat_q[:, cols], 1, 0)
        grad_pq = (grad_fq * slope_q[:, cols]).astype(BF16)
        grads[0, head_rows(head), :] = dot(turned_q[head_rows(head), :], grad_pq, 1, 0)

    def key_side(head):
        cols = head_rows(head)
        after = summed[1, head_rows(head), :].astype(BF16)
        grad_fk = dot(values[:, cols], after, 1, 1) + local_fk[:, cols]
        grad_pk = (grad_fk * slope_k[:, cols]).astype(BF16)
        grads[1, head_rows(head), :] = dot(turned_k[head_rows(head), :], grad_pk, 1, 0)

    def keys_pair(pair):
        both(key_features, pair)
        if pair == 0:
            pl.semaphore_wait(barrier, 1 + width - 1 + depth - 1)
        core_copy(0, pair).start()

    def forward_pair(pair):
        share_arrival(0, pair).wait_recv()
        both(forward, pair)
        core_copy(1, pair).start()

    def query_pair(pair):
        both(query_side, pair)
        reduce_start(0, pair)

    def key_pair(pair):
        share_arrival(1, pair).wait_recv()
        both(key_side, pair)
        reduce_start(1, pair)

    for one in loads[:3]:
        one.wait()
    keys_pair(0)
    keys_pair(1)
    scan_rows(0, 0)
    keys_pair(2)
    scan_rows(0, 1)
    keys_pair(3)
    scan_rows(0, 2)
    for one in loads[3:]:
        one.wait()
    gain_row[...] = gain[...].astype(F32).reshape(1, H * E)
    both(query_features, 0)
    scan_rows(0, 3)
    both(query_features, 1)
    scan_levels(0, 0, True)
    both(query_features, 2)
    scan_levels(0, 1, True)
    both(query_features, 3)
    scan_levels(0, 2, True)
    both(inside, 0)
    scan_levels(0, 3, True)
    both(inside, 1)
    scan_levels(0, 0, False)
    both(inside, 2)
    scan_levels(0, 1, False)
    both(inside, 3)
    scan_levels(0, 2, False)
    forward_pair(0)
    scan_levels(0, 3, False)
    forward_pair(1)
    scan_rows(1, 0)
    forward_pair(2)
    scan_rows(1, 1)
    scan_levels(1, 0, True)
    forward_pair(3)
    leave = pltpu.make_async_copy(attention, attention_hbm, store)
    leave.start()
    scan_rows(1, 2)
    scan_levels(1, 1, True)
    query_pair(0)
    scan_rows(1, 3)
    scan_levels(1, 2, True)
    query_pair(1)
    scan_levels(1, 3, True)
    reduce_rows(0, 0)
    query_pair(2)
    reduce_rows(0, 1)
    query_pair(3)
    scan_levels(1, 0, False)
    reduce_rows(0, 2)
    reduce_rows(0, 3)
    scan_levels(1, 1, False)
    for which in range(half // 2):
        reduce_levels(0, which)
    scan_levels(1, 2, False)
    for which in range(half // 2, half):
        reduce_levels(0, which)
    key_pair(0)
    scan_levels(1, 3, False)
    key_pair(1)
    reduce_rows(1, 0)
    update(0)
    key_pair(2)
    reduce_rows(1, 1)
    key_pair(3)
    reduce_rows(1, 2)
    reduce_rows(1, 3)
    for which in range(half):
        reduce_levels(1, which)
    spread(0)
    update(1)
    spread_core(0)
    spread(1)
    spread_core(1)
    spread_end(0)
    spread_end(1)
    scan_drain(0)
    scan_drain(1)
    drain(0)
    drain(1)
    leave.wait()


def hand_over(*refs):
    copies = [pltpu.make_async_copy(refs[i], refs[3 + i], refs[6].at[i]) for i in range(3)]
    for one in copies:
        one.start()
    for one in copies:
        one.wait()


def local(count, queries, keys, values, out_grad, maps, gain, first_moment, second_moment):
    depth, width = layout(count)
    half = depth // 2
    share = 2 * H * E // count
    tokens = queries.shape[0]
    wide = (SPAN, H * E)
    flat = (2 * H * E, E)
    square = (2, PAIRS, E, E)
    dma = pltpu.SemaphoreType.DMA
    chunks = half * width
    turned = (H * E, SPAN)
    scratch = [
        pltpu.VMEM(wide, BF16),
        pltpu.VMEM(wide, BF16),
        pltpu.VMEM(wide, BF16),
        pltpu.VMEM(wide, BF16),
        pltpu.VMEM(flat, F32),
        pltpu.VMEM((share, E), F32),
        pltpu.VMEM((share, E), F32),
        pltpu.VMEM((1, H * E), F32),
        pltpu.VMEM(wide, BF16),
        pltpu.VMEM(turned, BF16),
        pltpu.VMEM(turned, BF16),
        pltpu.VMEM(turned, BF16),
        pltpu.VMEM(wide, BF16),
        pltpu.VMEM(wide, BF16),
        pltpu.VMEM(wide, F32),
        pltpu.VMEM(wide, F32),
        pltpu.VMEM(wide, F32),
        pltpu.VMEM(wide, BF16),
        pltpu.VMEM(wide, F32),
        pltpu.VMEM((2, H * E, E), F32),
        pltpu.VMEM(square, F32),
        pltpu.VMEM(square, F32),
        pltpu.VMEM((2, width, PAIRS, E, E), F32),
        pltpu.VMEM(square, F32),
        pltpu.VMEM(square, F32),
        pltpu.VMEM(square, F32),
        pltpu.VMEM((2, H * E, E), F32),
        pltpu.VMEM((2, H * E, E), F32),
        pltpu.VMEM((2, chunks, share, E), F32),
        pltpu.VMEM((2, chunks, share, E), F32),
        pltpu.VMEM((2, half, width, share, E), F32),
        pltpu.VMEM((2, half, share, E), F32),
        pltpu.VMEM((depth, share, E), F32),
        dma((7,)),
        dma,
        dma((2, PAIRS)),
        dma((2, PAIRS)),
        dma((2, width, PAIRS)),
        dma((2, width, PAIRS)),
        dma((2, PAIRS)),
        dma((2, PAIRS)),
        dma((2, PAIRS)),
        dma((2, PAIRS)),
        dma((2, chunks)),
        dma((2, chunks)),
        dma((2, chunks)),
        dma((2, half, width)),
        dma((2, half)),
        dma((depth,)),
        dma((depth,)),
        dma((2, half)),
        dma((2, half, width)),
        dma((2, half, width)),
        dma((2, half, width)),
        dma((2, half, width)),
    ]
    vmem = pl.BlockSpec(memory_space=pltpu.VMEM)
    anywhere = pl.BlockSpec(memory_space=pl.ANY)
    attention, new_maps, new_moments = pl.pallas_call(
        functools.partial(kernel, depth, width, share),
        out_shape=(
            jax.ShapeDtypeStruct((tokens, H * E), BF16),
            jax.ShapeDtypeStruct(flat, F32),
            jax.ShapeDtypeStruct((2, share, E), F32),
        ),
        in_specs=[anywhere] * 7 + [vmem],
        out_specs=(anywhere, vmem, vmem),
        scratch_shapes=scratch,
        compiler_params=pltpu.CompilerParams(
            collective_id=0, has_side_effects=True, vmem_limit_bytes=60 * 1024 * 1024
        ),
        name="layer",
    )(
        queries, keys, values, out_grad, maps.reshape(flat),
        first_moment, second_moment, gain,
    )
    results = (attention, new_maps, new_moments)
    attention, new_maps, new_moments = pl.pallas_call(
        hand_over,
        out_shape=tuple(jax.ShapeDtypeStruct(one.shape, one.dtype) for one in results),
        in_specs=[anywhere] * 3,
        out_specs=(anywhere,) * 3,
        scratch_shapes=[dma((3,))],
        compiler_params=pltpu.CompilerParams(vmem_limit_bytes=63 * 1024 * 1024),
        name="results",
    )(*results)
    return attention, new_maps.reshape(2, H, E, E), new_moments


def solution(mesh):
    in_specs = (
        P(("groups", "seq"), None),
        P(("groups", "seq"), None),
        P(("groups", "seq"), None),
        P(("groups", "seq"), None),
        P(),
        P(),
        P("seq", None),
        P("seq", None),
    )
    out_specs = (
        P(("groups", "seq"), None),
        P("groups", None, None, None),
        P("groups", "seq", None),
    )
    return jax.shard_map(
        functools.partial(local, mesh.shape["seq"]),
        mesh=mesh, in_specs=in_specs, out_specs=out_specs, check_vma=False,
    )
```

```python
import functools

import jax
import jax.numpy as jnp
from jax import lax
from jax.experimental import pallas as pl
from jax.experimental.pallas import tpu as pltpu
from jax.sharding import PartitionSpec as P

H = 8
E = 128
SPAN = 256
OPT_STEP = 10
PAIRS = 4

BETA_ONE = 0.9
BETA_TWO = 0.95
RATE = 0.01
TINY = 1e-08
NORM_EPS = 1e-06

F32 = jnp.float32
BF16 = jnp.bfloat16


def dot(left, right, left_dim, right_dim):
    return lax.dot_general(
        left, right, (((left_dim,), (right_dim,)), ((), ())), preferred_element_type=F32
    )


def adam_rows(gradient, weights, first_old, second_old):
    first_new = BETA_ONE * first_old + (1.0 - BETA_ONE) * gradient
    second_new = BETA_TWO * second_old + (1.0 - BETA_TWO) * gradient * gradient
    first_hat = first_new / (1.0 - BETA_ONE**OPT_STEP)
    second_hat = second_new / (1.0 - BETA_TWO**OPT_STEP)
    return (weights - RATE * first_hat / (jnp.sqrt(second_hat) + TINY), first_new, second_new)


def layout(count):
    chips = count // 2
    row = 1
    while row * row * 4 <= chips:
        row *= 2
    return chips // row, row


def kernel(
    depth, width, share,
    queries_hbm, keys_hbm, values_hbm, out_grad_hbm, maps_hbm, first_hbm, second_hbm, gain,
    attention_hbm, new_maps, new_moments,
    queries, keys, values, out_grad, maps, first_old, second_old,
    gain_row, attention,
    feat_q, feat_k, slope_q, slope_k, raw_part, grad_raw, local_fk,
    states, core_in, chip, row_in, chain_in, chain_out, share_out, summed,
    grads, grads_core, grads_chip, grads_row, grads_part, rows_in,
    load, store,
    send_core, recv_core, send_row, recv_row, send_z, recv_z, send_share, recv_share,
    send_rc, recv_rc, send_ry, recv_ry, send_rz, recv_rz,
    send_gz, recv_gz, send_gy, recv_gy, send_gc, recv_gc,
):
    group = lax.axis_index("groups")
    me = lax.axis_index("seq")
    plane = 2 * width
    level = me // plane
    row = (me // 2) % width
    core = me % 2
    other_core = 1 - core
    half = depth // 2
    chunks = half * width
    per_pair = chunks // PAIRS
    rows_beside = [(row + step) % width for step in range(1, width)]
    levels = [(level + step) % depth for step in range(1, depth)]

    def index(to_level, to_row, to_core):
        return to_level * plane + to_row * 2 + to_core

    def remote(src, dst, send, recv, to_level, to_row, to_core):
        return pltpu.make_async_remote_copy(
            src_ref=src, dst_ref=dst, send_sem=send, recv_sem=recv,
            device_id=(group, index(to_level, to_row, to_core)),
            device_id_type=pl.DeviceIdType.MESH,
        )

    def span(start, size):
        return pl.ds(pl.multiple_of(start, size), size)

    def head_rows(head):
        return span(head * E, E)

    def greet(to):
        pl.semaphore_signal(
            barrier, inc=1, device_id=(group, to), device_id_type=pl.DeviceIdType.MESH
        )

    loads = [
        pltpu.make_async_copy(src, dst, load.at[slot])
        for slot, (src, dst) in enumerate(
            (
                (keys_hbm, keys),
                (maps_hbm, maps),
                (values_hbm, values),
                (queries_hbm, queries),
                (out_grad_hbm, out_grad),
                (first_hbm, first_old),
                (second_hbm, second_old),
            )
        )
    ]
    for one in loads:
        one.start()

    barrier = pltpu.get_barrier_semaphore()
    greet(index(level, row, other_core))
    for beside in rows_beside:
        greet(index(level, beside, core))
    for other in levels:
        greet(index(other, row, core))

    def masked(scores):
        line = lax.broadcasted_iota(jnp.int32, (SPAN, SPAN), 0)
        column = lax.broadcasted_iota(jnp.int32, (SPAN, SPAN), 1)
        return jnp.where(line >= column, scores, 0.0).astype(BF16)

    def both(body, pair):
        body(2 * pair)
        body(2 * pair + 1)

    def core_copy(way, pair):
        return remote(
            states.at[way, head_rows(2 * pair + other_core)], core_in.at[way, pair],
            send_core.at[way, pair], recv_core.at[way, pair], level, row, other_core,
        )

    def row_copy(way, pair, beside):
        return remote(
            chip.at[way, pair], row_in.at[way, row, pair],
            send_row.at[way, beside, pair], recv_row.at[way, row, pair], level, beside, core,
        )

    def row_arrival(way, pair, beside):
        return remote(
            chip.at[way, pair], row_in.at[way, beside, pair],
            send_row.at[way, row, pair], recv_row.at[way, beside, pair], level, beside, core,
        )

    def chain_copy(way, pair):
        return remote(
            chain_out.at[way, pair], chain_in.at[way, pair],
            send_z.at[way, pair], recv_z.at[way, pair],
            (level + (depth - 1 if way else 1)) % depth, row, core,
        )

    def share_copy(way, pair):
        mine = head_rows(2 * pair + core)
        return remote(
            share_out.at[way, pair], summed.at[way, mine],
            send_share.at[way, pair], recv_share.at[way, pair], level, row, other_core,
        )

    def share_arrival(way, pair):
        theirs = head_rows(2 * pair + other_core)
        return remote(
            share_out.at[way, pair], summed.at[way, theirs],
            send_share.at[way, pair], recv_share.at[way, pair], level, row, other_core,
        )

    def scan_rows(way, pair):
        core_copy(way, pair).wait_recv()
        own = states[way, head_rows(2 * pair + core), :]
        total = own + core_in[way, pair]
        chip[way, pair] = total
        for beside in rows_beside:
            row_copy(way, pair, beside).start()
        row_in[way, row, pair] = total

    def scan_levels(way, pair, first):
        last = 0 if way else depth - 1

        def steps():
            for beside in rows_beside:
                row_arrival(way, pair, beside).wait_recv()
            ahead = jnp.zeros((E, E), F32)
            total = jnp.zeros((E, E), F32)
            for member in range(width):
                one = row_in[way, member, pair]
                total = total + one
                counts = (member > row) if way else (member < row)
                ahead = ahead + jnp.where(counts, one, 0.0)
            if first:
                chain_out[way, pair] = total
                chain_copy(way, pair).start()
            else:
                chain_copy(way, pair).wait_recv()
                running = chain_in[way, pair]
                ahead = ahead + running

                @pl.when(level != last)
                def _():
                    chain_out[way, pair] = running + total
                    chain_copy(way, pair).start()

            near = core == (1 if way else 0)
            mine = head_rows(2 * pair + core)
            share_out[way, pair] = ahead + jnp.where(near, states[way, mine, :], 0.0)
            share_copy(way, pair).start()
            summed[way, mine, :] = ahead + jnp.where(near, 0.0, core_in[way, pair])

        at_first = level == (depth - 1 if way else 0)
        pl.when(at_first if first else jnp.logical_not(at_first))(steps)

    def scan_drain(way):
        last = 0 if way else depth - 1
        for pair in range(PAIRS):
            core_copy(way, pair).wait_send()
            share_copy(way, pair).wait_send()
            for beside in rows_beside:
                row_copy(way, pair, beside).wait_send()

            @pl.when(level != last)
            def _():
                chain_copy(way, pair).wait_send()

    def piece(chunk, of_core):
        return span((chunk * 2 + of_core) * share, share)

    def reduce_core_copy(side, chunk):
        return remote(
            grads.at[side, piece(chunk, other_core)], grads_core.at[side, chunk],
            send_rc.at[side, chunk], recv_rc.at[side, chunk], level, row, other_core,
        )

    def reduce_row_copy(side, chunk):
        which, to_row = chunk // width, chunk % width
        return remote(
            grads_chip.at[side, chunk], grads_row.at[side, which, row],
            send_ry.at[side, chunk], recv_ry.at[side, which, row], level, to_row, core,
        )

    def reduce_row_arrival(side, which, beside):
        return remote(
            grads_chip.at[side, 0], grads_row.at[side, which, beside],
            send_ry.at[side, 0], recv_ry.at[side, which, beside], level, beside, core,
        )

    def owner_copy(side, which):
        return remote(
            grads_part.at[side, which], rows_in.at[level],
            send_rz.at[side, which], recv_rz.at[level], side * half + which, row, core,
        )

    def owner_arrival(other):
        return remote(
            grads_part.at[0, 0], rows_in.at[other],
            send_rz.at[0, 0], recv_rz.at[other], other, row, core,
        )

    def reduce_start(side, pair):
        for chunk in range(pair * per_pair, (pair + 1) * per_pair):
            reduce_core_copy(side, chunk).start()

    def reduce_rows(side, pair):
        for chunk in range(pair * per_pair, (pair + 1) * per_pair):
            which, to_row = chunk // width, chunk % width
            reduce_core_copy(side, chunk).wait_recv()
            total = grads[side, piece(chunk, core), :] + grads_core[side, chunk]

            @pl.when(row == to_row)
            def _():
                grads_row[side, which, row] = total

            @pl.when(row != to_row)
            def _():
                grads_chip[side, chunk] = total
                reduce_row_copy(side, chunk).start()

    def reduce_levels(side, which):
        for beside in rows_beside:
            reduce_row_arrival(side, which, beside).wait_recv()
        total = grads_row[side, which, 0]
        for member in range(1, width):
            total = total + grads_row[side, which, member]

        @pl.when(level == side * half + which)
        def _():
            rows_in[level] = total

        @pl.when(level != side * half + which)
        def _():
            grads_part[side, which] = total
            owner_copy(side, which).start()

    def map_rows(of_level, of_row, of_core):
        return new_maps.at[span(index(of_level, of_row, of_core) * share, share)]

    def map_level_copy(side, other):
        mine = map_rows(level, row, core)
        return remote(
            mine, mine, send_gz.at[other], recv_gz.at[side, level - side * half],
            other, row, core,
        )

    def map_level_arrival(side, which):
        owner = side * half + which
        theirs = map_rows(owner, row, core)
        return remote(
            theirs, theirs, send_gz.at[owner], recv_gz.at[side, which], owner, row, core
        )

    def map_row_copy(side, which, beside):
        mine = map_rows(side * half + which, row, core)
        return remote(
            mine, mine, send_gy.at[side, which, beside], recv_gy.at[side, which, row],
            level, beside, core,
        )

    def map_row_arrival(side, which, beside):
        theirs = map_rows(side * half + which, beside, core)
        return remote(
            theirs, theirs, send_gy.at[side, which, row], recv_gy.at[side, which, beside],
            level, beside, core,
        )

    def map_core_copy(side, which, of_row):
        mine = map_rows(side * half + which, of_row, core)
        return remote(
            mine, mine, send_gc.at[side, which, of_row], recv_gc.at[side, which, of_row],
            level, row, other_core,
        )

    def map_core_arrival(side, which, of_row):
        theirs = map_rows(side * half + which, of_row, other_core)
        return remote(
            theirs, theirs, send_gc.at[side, which, of_row], recv_gc.at[side, which, of_row],
            level, row, other_core,
        )

    def update(side):
        @pl.when(level // half == side)
        def _():
            for other in levels:
                owner_arrival(other).wait_recv()
            gradient = rows_in[0]
            for other in range(1, depth):
                gradient = gradient + rows_in[other]
            mine = span(me * share, share)
            rows_new, first_new, second_new = adam_rows(
                gradient, maps[mine, :], first_old[...], second_old[...]
            )
            new_maps[mine, :] = rows_new
            for other in levels:
                map_level_copy(side, other).start()
            new_moments[0] = first_new
            new_moments[1] = second_new

    def spread(side):
        for which in range(half):

            @pl.when(level != side * half + which)
            def _():
                map_level_arrival(side, which).wait_recv()

            for beside in rows_beside:
                map_row_copy(side, which, beside).start()
            map_core_copy(side, which, row).start()

    def spread_core(side):
        for which in range(half):
            for beside in rows_beside:
                map_row_arrival(side, which, beside).wait_recv()
                map_core_copy(side, which, beside).start()

    def spread_end(side):
        for which in range(half):
            for of_row in range(width):
                map_core_arrival(side, which, of_row).wait_recv()

    def drain(side):
        for chunk in range(chunks):
            reduce_core_copy(side, chunk).wait_send()

            @pl.when(row != chunk % width)
            def _():
                reduce_row_copy(side, chunk).wait_send()

        for which in range(half):
            for beside in rows_beside:
                map_row_copy(side, which, beside).wait_send()
            for of_row in range(width):
                map_core_copy(side, which, of_row).wait_send()

            @pl.when(level != side * half + which)
            def _():
                owner_copy(side, which).wait_send()

        @pl.when(level // half == side)
        def _():
            for other in levels:
                map_level_copy(side, other).wait_send()

    def feature(source, weights, feat, slope, cols):
        pre = dot(source[:, cols], weights.astype(BF16), 1, 0)
        sigmoid = 1.0 / (1.0 + jnp.exp(-pre))
        feat[:, cols] = (pre * sigmoid).astype(BF16)
        slope[:, cols] = sigmoid * (1.0 + pre * (1.0 - sigmoid))

    def key_features(head):
        cols = head_rows(head)
        feature(keys, maps[head_rows(H + head), :], feat_k, slope_k, cols)
        states[0, head_rows(head), :] = dot(feat_k[:, cols], values[:, cols], 0, 0)

    def query_features(head):
        cols = head_rows(head)
        feature(queries, maps[head_rows(head), :], feat_q, slope_q, cols)

    def inside(head):
        cols = head_rows(head)
        scores = masked(dot(feat_q[:, cols], feat_k[:, cols], 1, 1))
        raw_part[:, cols] = dot(scores, values[:, cols], 1, 0)

    def forward(head):
        cols = head_rows(head)
        before = summed[0, head_rows(head), :].astype(BF16)
        raw = dot(feat_q[:, cols], before, 1, 0) + raw_part[:, cols]
        scale = lax.rsqrt(jnp.mean(raw * raw, -1, keepdims=True) + NORM_EPS)
        unit = raw * scale
        wide = gain_row[:, cols]
        attention[:, cols] = (unit * wide).astype(BF16)
        dunit = out_grad[:, cols].astype(F32) * wide
        inner = jnp.mean(dunit * unit, -1, keepdims=True)
        grad = (scale * (dunit - unit * inner)).astype(BF16)
        grad_raw[:, cols] = grad
        states[1, head_rows(head), :] = dot(feat_q[:, cols], grad, 0, 0)

    def query_side(head):
        cols = head_rows(head)
        grad = grad_raw[:, cols]
        pscores = masked(dot(grad, values[:, cols], 1, 1))
        before = summed[0, head_rows(head), :].astype(BF16)
        grad_fq = dot(grad, before, 1, 1) + dot(pscores, feat_k[:, cols], 1, 0)
        local_fk[:, cols] = dot(pscores, feat_q[:, cols], 0, 0)
        grad_pq = (grad_fq * slope_q[:, cols]).astype(BF16)
        grads[0, head_rows(head), :] = dot(queries[:, cols], grad_pq, 0, 0)

    def key_side(head):
        cols = head_rows(head)
        after = summed[1, head_rows(head), :].astype(BF16)
        grad_fk = dot(values[:, cols], after, 1, 1) + local_fk[:, cols]
        grad_pk = (grad_fk * slope_k[:, cols]).astype(BF16)
        grads[1, head_rows(head), :] = dot(keys[:, cols], grad_pk, 0, 0)

    def keys_pair(pair):
        both(key_features, pair)
        if pair == 0:
            pl.semaphore_wait(barrier, 1 + width - 1 + depth - 1)
        core_copy(0, pair).start()

    def forward_pair(pair):
        share_arrival(0, pair).wait_recv()
        both(forward, pair)
        core_copy(1, pair).start()

    def query_pair(pair):
        both(query_side, pair)
        reduce_start(0, pair)

    def key_pair(pair):
        share_arrival(1, pair).wait_recv()
        both(key_side, pair)
        reduce_start(1, pair)

    for one in loads[:3]:
        one.wait()
    keys_pair(0)
    keys_pair(1)
    scan_rows(0, 0)
    keys_pair(2)
    scan_rows(0, 1)
    keys_pair(3)
    scan_rows(0, 2)
    for one in loads[3:]:
        one.wait()
    gain_row[...] = gain[...].astype(F32).reshape(1, H * E)
    both(query_features, 0)
    scan_rows(0, 3)
    both(query_features, 1)
    scan_levels(0, 0, True)
    both(query_features, 2)
    scan_levels(0, 1, True)
    both(query_features, 3)
    scan_levels(0, 2, True)
    both(inside, 0)
    scan_levels(0, 3, True)
    both(inside, 1)
    scan_levels(0, 0, False)
    both(inside, 2)
    scan_levels(0, 1, False)
    both(inside, 3)
    scan_levels(0, 2, False)
    forward_pair(0)
    scan_levels(0, 3, False)
    forward_pair(1)
    scan_rows(1, 0)
    forward_pair(2)
    scan_rows(1, 1)
    scan_levels(1, 0, True)
    forward_pair(3)
    leave = pltpu.make_async_copy(attention, attention_hbm, store)
    leave.start()
    scan_rows(1, 2)
    scan_levels(1, 1, True)
    query_pair(0)
    scan_rows(1, 3)
    scan_levels(1, 2, True)
    query_pair(1)
    scan_levels(1, 3, True)
    reduce_rows(0, 0)
    query_pair(2)
    reduce_rows(0, 1)
    query_pair(3)
    scan_levels(1, 0, False)
    reduce_rows(0, 2)
    reduce_rows(0, 3)
    scan_levels(1, 1, False)
    for which in range(half // 2):
        reduce_levels(0, which)
    scan_levels(1, 2, False)
    for which in range(half // 2, half):
        reduce_levels(0, which)
    key_pair(0)
    scan_levels(1, 3, False)
    key_pair(1)
    reduce_rows(1, 0)
    update(0)
    key_pair(2)
    reduce_rows(1, 1)
    key_pair(3)
    reduce_rows(1, 2)
    reduce_rows(1, 3)
    for which in range(half):
        reduce_levels(1, which)
    spread(0)
    update(1)
    spread_core(0)
    spread(1)
    spread_core(1)
    spread_end(0)
    spread_end(1)
    scan_drain(0)
    scan_drain(1)
    drain(0)
    drain(1)
    leave.wait()


def hand_over(sources, targets, staged, arrive, leave):
    moves = []
    for source, target, stage in zip(sources, targets, staged):
        rows = source.shape[0]
        size = min(rows, max(rows // 4, SPAN // 2))
        for start in range(0, rows, size):
            here = pl.ds(start, size)
            slot = len(moves)
            moves.append((
                pltpu.make_async_copy(source.at[here], stage.at[here], arrive.at[slot]),
                pltpu.make_async_copy(stage.at[here], target.at[here], leave.at[slot]),
            ))
    for into, _ in moves:
        into.start()
    for into, out in moves:
        into.wait()
        out.start()
    for _, out in moves:
        out.wait()


def local(count, queries, keys, values, out_grad, maps, gain, first_moment, second_moment):
    depth, width = layout(count)
    half = depth // 2
    share = 2 * H * E // count
    tokens = queries.shape[0]
    wide = (SPAN, H * E)
    flat = (2 * H * E, E)
    square = (2, PAIRS, E, E)
    dma = pltpu.SemaphoreType.DMA
    chunks = half * width
    scratch = [
        pltpu.VMEM(wide, BF16),
        pltpu.VMEM(wide, BF16),
        pltpu.VMEM(wide, BF16),
        pltpu.VMEM(wide, BF16),
        pltpu.VMEM(flat, F32),
        pltpu.VMEM((share, E), F32),
        pltpu.VMEM((share, E), F32),
        pltpu.VMEM((1, H * E), F32),
        pltpu.VMEM(wide, BF16),
        pltpu.VMEM(wide, BF16),
        pltpu.VMEM(wide, BF16),
        pltpu.VMEM(wide, F32),
        pltpu.VMEM(wide, F32),
        pltpu.VMEM(wide, F32),
        pltpu.VMEM(wide, BF16),
        pltpu.VMEM(wide, F32),
        pltpu.VMEM((2, H * E, E), F32),
        pltpu.VMEM(square, F32),
        pltpu.VMEM(square, F32),
        pltpu.VMEM((2, width, PAIRS, E, E), F32),
        pltpu.VMEM(square, F32),
        pltpu.VMEM(square, F32),
        pltpu.VMEM(square, F32),
        pltpu.VMEM((2, H * E, E), F32),
        pltpu.VMEM((2, H * E, E), F32),
        pltpu.VMEM((2, chunks, share, E), F32),
        pltpu.VMEM((2, chunks, share, E), F32),
        pltpu.VMEM((2, half, width, share, E), F32),
        pltpu.VMEM((2, half, share, E), F32),
        pltpu.VMEM((depth, share, E), F32),
        dma((7,)),
        dma,
        dma((2, PAIRS)),
        dma((2, PAIRS)),
        dma((2, width, PAIRS)),
        dma((2, width, PAIRS)),
        dma((2, PAIRS)),
        dma((2, PAIRS)),
        dma((2, PAIRS)),
        dma((2, PAIRS)),
        dma((2, chunks)),
        dma((2, chunks)),
        dma((2, chunks)),
        dma((2, half, width)),
        dma((2, half)),
        dma((depth,)),
        dma((depth,)),
        dma((2, half)),
        dma((2, half, width)),
        dma((2, half, width)),
        dma((2, half, width)),
        dma((2, half, width)),
    ]
    vmem = pl.BlockSpec(memory_space=pltpu.VMEM)
    anywhere = pl.BlockSpec(memory_space=pl.ANY)
    attention, new_maps, new_moments = pl.pallas_call(
        functools.partial(kernel, depth, width, share),
        out_shape=(
            jax.ShapeDtypeStruct((tokens, H * E), BF16),
            jax.ShapeDtypeStruct(flat, F32),
            jax.ShapeDtypeStruct((2, share, E), F32),
        ),
        in_specs=[anywhere] * 7 + [vmem],
        out_specs=(anywhere, vmem, vmem),
        scratch_shapes=scratch,
        compiler_params=pltpu.CompilerParams(
            collective_id=0, has_side_effects=True, vmem_limit_bytes=60 * 1024 * 1024
        ),
        name="layer",
    )(
        queries, keys, values, out_grad, maps.reshape(flat),
        first_moment, second_moment, gain,
    )
    results = (attention, new_maps, new_moments)
    attention, new_maps, new_moments = pl.pallas_call(
        lambda *refs: hand_over(refs[:3], refs[3:6], refs[6:9], *refs[9:]),
        out_shape=tuple(jax.ShapeDtypeStruct(one.shape, one.dtype) for one in results),
        in_specs=[anywhere] * 3,
        out_specs=(anywhere,) * 3,
        scratch_shapes=[pltpu.VMEM(one.shape, one.dtype) for one in results]
        + [dma((8,)), dma((8,))],
        compiler_params=pltpu.CompilerParams(vmem_limit_bytes=63 * 1024 * 1024),
        name="results",
    )(*results)
    return attention, new_maps.reshape(2, H, E, E), new_moments


def solution(mesh):
    in_specs = (
        P(("groups", "seq"), None),
        P(("groups", "seq"), None),
        P(("groups", "seq"), None),
        P(("groups", "seq"), None),
        P(),
        P(),
        P("seq", None),
        P("seq", None),
    )
    out_specs = (
        P(("groups", "seq"), None),
        P("groups", None, None, None),
        P("groups", "seq", None),
    )
    return jax.shard_map(
        functools.partial(local, mesh.shape["seq"]),
        mesh=mesh, in_specs=in_specs, out_specs=out_specs, check_vma=False,
    )
```

```python
import functools

import jax
import jax.numpy as jnp
from jax import lax
from jax.experimental import pallas as pl
from jax.experimental.pallas import tpu as pltpu
from jax.sharding import PartitionSpec as P

H = 8
E = 128
SPAN = 256
OPT_STEP = 10
PAIRS = 4

BETA_ONE = 0.9
BETA_TWO = 0.95
RATE = 0.01
TINY = 1e-08
NORM_EPS = 1e-06

F32 = jnp.float32
BF16 = jnp.bfloat16


def dot(left, right, left_dim, right_dim):
    return lax.dot_general(
        left, right, (((left_dim,), (right_dim,)), ((), ())), preferred_element_type=F32
    )


def adam_rows(gradient, weights, first_old, second_old):
    first_new = BETA_ONE * first_old + (1.0 - BETA_ONE) * gradient
    second_new = BETA_TWO * second_old + (1.0 - BETA_TWO) * gradient * gradient
    first_hat = first_new / (1.0 - BETA_ONE**OPT_STEP)
    second_hat = second_new / (1.0 - BETA_TWO**OPT_STEP)
    return (weights - RATE * first_hat / (jnp.sqrt(second_hat) + TINY), first_new, second_new)


def layout(count):
    chips = count // 2
    row = 1
    while row * row * 4 <= chips:
        row *= 2
    return chips // row, row


def kernel(
    depth, width, share,
    queries_hbm, keys_hbm, values_hbm, out_grad_hbm, maps_hbm, first_hbm, second_hbm, gain,
    attention_hbm, new_maps, new_moments,
    queries, keys, values, out_grad, maps, first_old, second_old,
    gain_row, attention,
    feat_q, feat_k, slope_q, slope_k, raw_part, grad_raw, local_fk,
    states, core_in, chip, row_in, chain_in, chain_out, share_out, summed,
    grads, grads_core, grads_chip, grads_row, grads_part, rows_in,
    load, store,
    send_core, recv_core, send_row, recv_row, send_z, recv_z, send_share, recv_share,
    send_rc, recv_rc, send_ry, recv_ry, send_rz, recv_rz,
    send_gz, recv_gz, send_gy, recv_gy, send_gc, recv_gc,
):
    group = lax.axis_index("groups")
    me = lax.axis_index("seq")
    plane = 2 * width
    level = me // plane
    row = (me // 2) % width
    core = me % 2
    other_core = 1 - core
    half = depth // 2
    chunks = half * width
    per_pair = chunks // PAIRS
    rows_beside = [(row + step) % width for step in range(1, width)]
    levels = [(level + step) % depth for step in range(1, depth)]

    def index(to_level, to_row, to_core):
        return to_level * plane + to_row * 2 + to_core

    def remote(src, dst, send, recv, to_level, to_row, to_core):
        return pltpu.make_async_remote_copy(
            src_ref=src, dst_ref=dst, send_sem=send, recv_sem=recv,
            device_id=(group, index(to_level, to_row, to_core)),
            device_id_type=pl.DeviceIdType.MESH,
        )

    def span(start, size):
        return pl.ds(pl.multiple_of(start, size), size)

    def head_rows(head):
        return span(head * E, E)

    def greet(to):
        pl.semaphore_signal(
            barrier, inc=1, device_id=(group, to), device_id_type=pl.DeviceIdType.MESH
        )

    loads = [
        pltpu.make_async_copy(src, dst, load.at[slot])
        for slot, (src, dst) in enumerate(
            (
                (keys_hbm, keys),
                (maps_hbm, maps),
                (values_hbm, values),
                (queries_hbm, queries),
                (out_grad_hbm, out_grad),
                (first_hbm, first_old),
                (second_hbm, second_old),
            )
        )
    ]
    for one in loads:
        one.start()

    barrier = pltpu.get_barrier_semaphore()
    greet(index(level, row, other_core))
    for beside in rows_beside:
        greet(index(level, beside, core))
    for other in levels:
        greet(index(other, row, core))

    def masked(scores):
        line = lax.broadcasted_iota(jnp.int32, (SPAN, SPAN), 0)
        column = lax.broadcasted_iota(jnp.int32, (SPAN, SPAN), 1)
        return jnp.where(line >= column, scores, 0.0).astype(BF16)

    def both(body, pair):
        body(2 * pair)
        body(2 * pair + 1)

    def core_copy(way, pair):
        return remote(
            states.at[way, head_rows(2 * pair + other_core)], core_in.at[way, pair],
            send_core.at[way, pair], recv_core.at[way, pair], level, row, other_core,
        )

    def row_copy(way, pair, beside):
        return remote(
            chip.at[way, pair], row_in.at[way, row, pair],
            send_row.at[way, beside, pair], recv_row.at[way, row, pair], level, beside, core,
        )

    def row_arrival(way, pair, beside):
        return remote(
            chip.at[way, pair], row_in.at[way, beside, pair],
            send_row.at[way, row, pair], recv_row.at[way, beside, pair], level, beside, core,
        )

    def chain_copy(way, pair):
        return remote(
            chain_out.at[way, pair], chain_in.at[way, pair],
            send_z.at[way, pair], recv_z.at[way, pair],
            (level + (depth - 1 if way else 1)) % depth, row, core,
        )

    def share_copy(way, pair):
        mine = head_rows(2 * pair + core)
        return remote(
            share_out.at[way, pair], summed.at[way, mine],
            send_share.at[way, pair], recv_share.at[way, pair], level, row, other_core,
        )

    def share_arrival(way, pair):
        theirs = head_rows(2 * pair + other_core)
        return remote(
            share_out.at[way, pair], summed.at[way, theirs],
            send_share.at[way, pair], recv_share.at[way, pair], level, row, other_core,
        )

    def scan_rows(way, pair):
        core_copy(way, pair).wait_recv()
        own = states[way, head_rows(2 * pair + core), :]
        total = own + core_in[way, pair]
        chip[way, pair] = total
        for beside in rows_beside:
            row_copy(way, pair, beside).start()
        row_in[way, row, pair] = total

    def scan_levels(way, pair, first):
        last = 0 if way else depth - 1

        def steps():
            for beside in rows_beside:
                row_arrival(way, pair, beside).wait_recv()
            ahead = jnp.zeros((E, E), F32)
            total = jnp.zeros((E, E), F32)
            for member in range(width):
                one = row_in[way, member, pair]
                total = total + one
                counts = (member > row) if way else (member < row)
                ahead = ahead + jnp.where(counts, one, 0.0)
            if first:
                chain_out[way, pair] = total
                chain_copy(way, pair).start()
            else:
                chain_copy(way, pair).wait_recv()
                running = chain_in[way, pair]
                ahead = ahead + running

                @pl.when(level != last)
                def _():
                    chain_out[way, pair] = running + total
                    chain_copy(way, pair).start()

            near = core == (1 if way else 0)
            mine = head_rows(2 * pair + core)
            share_out[way, pair] = ahead + jnp.where(near, states[way, mine, :], 0.0)
            share_copy(way, pair).start()
            summed[way, mine, :] = ahead + jnp.where(near, 0.0, core_in[way, pair])

        at_first = level == (depth - 1 if way else 0)
        pl.when(at_first if first else jnp.logical_not(at_first))(steps)

    def scan_drain(way):
        last = 0 if way else depth - 1
        for pair in range(PAIRS):
            core_copy(way, pair).wait_send()
            share_copy(way, pair).wait_send()
            for beside in rows_beside:
                row_copy(way, pair, beside).wait_send()

            @pl.when(level != last)
            def _():
                chain_copy(way, pair).wait_send()

    def piece(chunk, of_core):
        return span((chunk * 2 + of_core) * share, share)

    def reduce_core_copy(side, chunk):
        return remote(
            grads.at[side, piece(chunk, other_core)], grads_core.at[side, chunk],
            send_rc.at[side, chunk], recv_rc.at[side, chunk], level, row, other_core,
        )

    def reduce_row_copy(side, chunk):
        which, to_row = chunk // width, chunk % width
        return remote(
            grads_chip.at[side, chunk], grads_row.at[side, which, row],
            send_ry.at[side, chunk], recv_ry.at[side, which, row], level, to_row, core,
        )

    def reduce_row_arrival(side, which, beside):
        return remote(
            grads_chip.at[side, 0], grads_row.at[side, which, beside],
            send_ry.at[side, 0], recv_ry.at[side, which, beside], level, beside, core,
        )

    def owner_copy(side, which):
        return remote(
            grads_part.at[side, which], rows_in.at[level],
            send_rz.at[side, which], recv_rz.at[level], side * half + which, row, core,
        )

    def owner_arrival(other):
        return remote(
            grads_part.at[0, 0], rows_in.at[other],
            send_rz.at[0, 0], recv_rz.at[other], other, row, core,
        )

    def reduce_start(side, pair):
        for chunk in range(pair * per_pair, (pair + 1) * per_pair):
            reduce_core_copy(side, chunk).start()

    def reduce_rows(side, pair):
        for chunk in range(pair * per_pair, (pair + 1) * per_pair):
            which, to_row = chunk // width, chunk % width
            reduce_core_copy(side, chunk).wait_recv()
            total = grads[side, piece(chunk, core), :] + grads_core[side, chunk]

            @pl.when(row == to_row)
            def _():
                grads_row[side, which, row] = total

            @pl.when(row != to_row)
            def _():
                grads_chip[side, chunk] = total
                reduce_row_copy(side, chunk).start()

    def reduce_levels(side, which):
        for beside in rows_beside:
            reduce_row_arrival(side, which, beside).wait_recv()
        total = grads_row[side, which, 0]
        for member in range(1, width):
            total = total + grads_row[side, which, member]

        @pl.when(level == side * half + which)
        def _():
            rows_in[level] = total

        @pl.when(level != side * half + which)
        def _():
            grads_part[side, which] = total
            owner_copy(side, which).start()

    def map_rows(of_level, of_row, of_core):
        return new_maps.at[span(index(of_level, of_row, of_core) * share, share)]

    def map_level_copy(side, other):
        mine = map_rows(level, row, core)
        return remote(
            mine, mine, send_gz.at[other], recv_gz.at[side, level - side * half],
            other, row, core,
        )

    def map_level_arrival(side, which):
        owner = side * half + which
        theirs = map_rows(owner, row, core)
        return remote(
            theirs, theirs, send_gz.at[owner], recv_gz.at[side, which], owner, row, core
        )

    def map_row_copy(side, which, beside):
        mine = map_rows(side * half + which, row, core)
        return remote(
            mine, mine, send_gy.at[side, which, beside], recv_gy.at[side, which, row],
            level, beside, core,
        )

    def map_row_arrival(side, which, beside):
        theirs = map_rows(side * half + which, beside, core)
        return remote(
            theirs, theirs, send_gy.at[side, which, row], recv_gy.at[side, which, beside],
            level, beside, core,
        )

    def map_core_copy(side, which, of_row):
        mine = map_rows(side * half + which, of_row, core)
        return remote(
            mine, mine, send_gc.at[side, which, of_row], recv_gc.at[side, which, of_row],
            level, row, other_core,
        )

    def map_core_arrival(side, which, of_row):
        theirs = map_rows(side * half + which, of_row, other_core)
        return remote(
            theirs, theirs, send_gc.at[side, which, of_row], recv_gc.at[side, which, of_row],
            level, row, other_core,
        )

    def update(side):
        @pl.when(level // half == side)
        def _():
            for other in levels:
                owner_arrival(other).wait_recv()
            gradient = rows_in[0]
            for other in range(1, depth):
                gradient = gradient + rows_in[other]
            mine = span(me * share, share)
            rows_new, first_new, second_new = adam_rows(
                gradient, maps[mine, :], first_old[...], second_old[...]
            )
            new_maps[mine, :] = rows_new
            if side == 0:
                for which in range(half):
                    owner_copy(1, which).wait_send()
            for other in levels:
                map_level_copy(side, other).start()
            own = level - side * half
            for beside in rows_beside:
                map_row_copy(side, own, beside).start()
            map_core_copy(side, own, row).start()
            new_moments[0] = first_new
            new_moments[1] = second_new

    def spread(side):
        for which in range(half):

            @pl.when(level != side * half + which)
            def _():
                map_level_arrival(side, which).wait_recv()
                for beside in rows_beside:
                    map_row_copy(side, which, beside).start()
                map_core_copy(side, which, row).start()

    def spread_core(side):
        for which in range(half):
            for beside in rows_beside:
                map_row_arrival(side, which, beside).wait_recv()
                map_core_copy(side, which, beside).start()

    def spread_end(side):
        for which in range(half):
            for of_row in range(width):
                map_core_arrival(side, which, of_row).wait_recv()

    def drain(side):
        for chunk in range(chunks):
            reduce_core_copy(side, chunk).wait_send()

            @pl.when(row != chunk % width)
            def _():
                reduce_row_copy(side, chunk).wait_send()

        for which in range(half):
            for beside in rows_beside:
                map_row_copy(side, which, beside).wait_send()
            for of_row in range(width):
                map_core_copy(side, which, of_row).wait_send()

            passed = level != side * half + which
            if side == 1:
                passed = jnp.logical_and(passed, level >= half)

            @pl.when(passed)
            def _():
                owner_copy(side, which).wait_send()

        @pl.when(level // half == side)
        def _():
            for other in levels:
                map_level_copy(side, other).wait_send()

    def feature(source, weights, feat, slope, cols):
        pre = dot(source[:, cols], weights.astype(BF16), 1, 0)
        sigmoid = 1.0 / (1.0 + jnp.exp(-pre))
        feat[:, cols] = (pre * sigmoid).astype(BF16)
        slope[:, cols] = sigmoid * (1.0 + pre * (1.0 - sigmoid))

    def key_features(head):
        cols = head_rows(head)
        feature(keys, maps[head_rows(H + head), :], feat_k, slope_k, cols)
        states[0, head_rows(head), :] = dot(feat_k[:, cols], values[:, cols], 0, 0)

    def query_features(head):
        cols = head_rows(head)
        feature(queries, maps[head_rows(head), :], feat_q, slope_q, cols)

    def inside(head):
        cols = head_rows(head)
        scores = masked(dot(feat_q[:, cols], feat_k[:, cols], 1, 1))
        raw_part[:, cols] = dot(scores, values[:, cols], 1, 0)

    def forward(head):
        cols = head_rows(head)
        before = summed[0, head_rows(head), :].astype(BF16)
        raw = dot(feat_q[:, cols], before, 1, 0) + raw_part[:, cols]
        scale = lax.rsqrt(jnp.mean(raw * raw, -1, keepdims=True) + NORM_EPS)
        unit = raw * scale
        wide = gain_row[:, cols]
        attention[:, cols] = (unit * wide).astype(BF16)
        dunit = out_grad[:, cols].astype(F32) * wide
        inner = jnp.mean(dunit * unit, -1, keepdims=True)
        grad = (scale * (dunit - unit * inner)).astype(BF16)
        grad_raw[:, cols] = grad
        states[1, head_rows(head), :] = dot(feat_q[:, cols], grad, 0, 0)

    def query_side(head):
        cols = head_rows(head)
        grad = grad_raw[:, cols]
        pscores = masked(dot(grad, values[:, cols], 1, 1))
        before = summed[0, head_rows(head), :].astype(BF16)
        grad_fq = dot(grad, before, 1, 1) + dot(pscores, feat_k[:, cols], 1, 0)
        local_fk[:, cols] = dot(pscores, feat_q[:, cols], 0, 0)
        grad_pq = (grad_fq * slope_q[:, cols]).astype(BF16)
        grads[0, head_rows(head), :] = dot(queries[:, cols], grad_pq, 0, 0)

    def key_side(head):
        cols = head_rows(head)
        after = summed[1, head_rows(head), :].astype(BF16)
        grad_fk = dot(values[:, cols], after, 1, 1) + local_fk[:, cols]
        grad_pk = (grad_fk * slope_k[:, cols]).astype(BF16)
        grads[1, head_rows(head), :] = dot(keys[:, cols], grad_pk, 0, 0)

    def keys_pair(pair):
        both(key_features, pair)
        if pair == 0:
            pl.semaphore_wait(barrier, 1 + width - 1 + depth - 1)
        core_copy(0, pair).start()

    def forward_pair(pair):
        share_arrival(0, pair).wait_recv()
        both(forward, pair)
        core_copy(1, pair).start()

    def query_pair(pair):
        both(query_side, pair)
        reduce_start(0, pair)

    def reduce_queries():
        for which in range(half):
            reduce_levels(0, which)

    def key_pair(pair):
        share_arrival(1, pair).wait_recv()
        both(key_side, pair)
        reduce_start(1, pair)

    for one in loads[:3]:
        one.wait()
    keys_pair(0)
    keys_pair(1)
    scan_rows(0, 0)
    keys_pair(2)
    scan_rows(0, 1)
    keys_pair(3)
    scan_rows(0, 2)
    for one in loads[3:]:
        one.wait()
    gain_row[...] = gain[...].astype(F32).reshape(1, H * E)
    both(query_features, 0)
    scan_rows(0, 3)
    both(query_features, 1)
    scan_levels(0, 0, True)
    both(query_features, 2)
    scan_levels(0, 1, True)
    both(query_features, 3)
    scan_levels(0, 2, True)
    both(inside, 0)
    scan_levels(0, 3, True)
    both(inside, 1)
    scan_levels(0, 0, False)
    both(inside, 2)
    scan_levels(0, 1, False)
    both(inside, 3)
    scan_levels(0, 2, False)
    forward_pair(0)
    scan_levels(0, 3, False)
    forward_pair(1)
    scan_rows(1, 0)
    forward_pair(2)
    scan_rows(1, 1)
    forward_pair(3)
    leave = pltpu.make_async_copy(attention, attention_hbm, store)
    leave.start()
    scan_rows(1, 2)
    scan_levels(1, 0, True)
    query_pair(0)
    scan_rows(1, 3)
    scan_levels(1, 1, True)
    query_pair(1)
    scan_levels(1, 2, True)
    query_pair(2)
    scan_levels(1, 3, True)
    query_pair(3)
    for pair in range(PAIRS):
        reduce_rows(0, pair)
    pl.when(level < half)(reduce_queries)
    scan_levels(1, 0, False)
    scan_levels(1, 1, False)
    scan_levels(1, 2, False)
    key_pair(0)
    scan_levels(1, 3, False)
    pl.when(level >= half)(reduce_queries)
    key_pair(1)
    reduce_rows(1, 0)
    key_pair(2)
    reduce_rows(1, 1)
    key_pair(3)
    reduce_rows(1, 2)
    reduce_rows(1, 3)
    for which in range(half):
        reduce_levels(1, which)
    update(0)
    update(1)
    spread(0)
    spread_core(0)
    spread(1)
    spread_core(1)
    spread_end(0)
    spread_end(1)
    scan_drain(0)
    scan_drain(1)
    drain(0)
    drain(1)
    leave.wait()


def hand_over(sources, targets, staged, arrive, leave):
    moves = []
    for source, target, stage in zip(sources, targets, staged):
        rows = source.shape[0]
        size = min(rows, max(rows // 4, SPAN // 2))
        for start in range(0, rows, size):
            here = pl.ds(start, size)
            slot = len(moves)
            moves.append((
                pltpu.make_async_copy(source.at[here], stage.at[here], arrive.at[slot]),
                pltpu.make_async_copy(stage.at[here], target.at[here], leave.at[slot]),
            ))
    for into, _ in moves:
        into.start()
    for into, out in moves:
        into.wait()
        out.start()
    for _, out in moves:
        out.wait()


def local(count, queries, keys, values, out_grad, maps, gain, first_moment, second_moment):
    depth, width = layout(count)
    half = depth // 2
    share = 2 * H * E // count
    tokens = queries.shape[0]
    wide = (SPAN, H * E)
    flat = (2 * H * E, E)
    square = (2, PAIRS, E, E)
    dma = pltpu.SemaphoreType.DMA
    chunks = half * width
    scratch = [
        pltpu.VMEM(wide, BF16),
        pltpu.VMEM(wide, BF16),
        pltpu.VMEM(wide, BF16),
        pltpu.VMEM(wide, BF16),
        pltpu.VMEM(flat, F32),
        pltpu.VMEM((share, E), F32),
        pltpu.VMEM((share, E), F32),
        pltpu.VMEM((1, H * E), F32),
        pltpu.VMEM(wide, BF16),
        pltpu.VMEM(wide, BF16),
        pltpu.VMEM(wide, BF16),
        pltpu.VMEM(wide, F32),
        pltpu.VMEM(wide, F32),
        pltpu.VMEM(wide, F32),
        pltpu.VMEM(wide, BF16),
        pltpu.VMEM(wide, F32),
        pltpu.VMEM((2, H * E, E), F32),
        pltpu.VMEM(square, F32),
        pltpu.VMEM(square, F32),
        pltpu.VMEM((2, width, PAIRS, E, E), F32),
        pltpu.VMEM(square, F32),
        pltpu.VMEM(square, F32),
        pltpu.VMEM(square, F32),
        pltpu.VMEM((2, H * E, E), F32),
        pltpu.VMEM((2, H * E, E), F32),
        pltpu.VMEM((2, chunks, share, E), F32),
        pltpu.VMEM((2, chunks, share, E), F32),
        pltpu.VMEM((2, half, width, share, E), F32),
        pltpu.VMEM((2, half, share, E), F32),
        pltpu.VMEM((depth, share, E), F32),
        dma((7,)),
        dma,
        dma((2, PAIRS)),
        dma((2, PAIRS)),
        dma((2, width, PAIRS)),
        dma((2, width, PAIRS)),
        dma((2, PAIRS)),
        dma((2, PAIRS)),
        dma((2, PAIRS)),
        dma((2, PAIRS)),
        dma((2, chunks)),
        dma((2, chunks)),
        dma((2, chunks)),
        dma((2, half, width)),
        dma((2, half)),
        dma((depth,)),
        dma((depth,)),
        dma((2, half)),
        dma((2, half, width)),
        dma((2, half, width)),
        dma((2, half, width)),
        dma((2, half, width)),
    ]
    vmem = pl.BlockSpec(memory_space=pltpu.VMEM)
    anywhere = pl.BlockSpec(memory_space=pl.ANY)
    attention, new_maps, new_moments = pl.pallas_call(
        functools.partial(kernel, depth, width, share),
        out_shape=(
            jax.ShapeDtypeStruct((tokens, H * E), BF16),
            jax.ShapeDtypeStruct(flat, F32),
            jax.ShapeDtypeStruct((2, share, E), F32),
        ),
        in_specs=[anywhere] * 7 + [vmem],
        out_specs=(anywhere, vmem, vmem),
        scratch_shapes=scratch,
        compiler_params=pltpu.CompilerParams(
            collective_id=0, has_side_effects=True, vmem_limit_bytes=60 * 1024 * 1024
        ),
        name="layer",
    )(
        queries, keys, values, out_grad, maps.reshape(flat),
        first_moment, second_moment, gain,
    )
    results = (attention, new_maps, new_moments)
    attention, new_maps, new_moments = pl.pallas_call(
        lambda *refs: hand_over(refs[:3], refs[3:6], refs[6:9], *refs[9:]),
        out_shape=tuple(jax.ShapeDtypeStruct(one.shape, one.dtype) for one in results),
        in_specs=[anywhere] * 3,
        out_specs=(anywhere,) * 3,
        scratch_shapes=[pltpu.VMEM(one.shape, one.dtype) for one in results]
        + [dma((8,)), dma((8,))],
        compiler_params=pltpu.CompilerParams(vmem_limit_bytes=63 * 1024 * 1024),
        name="results",
    )(*results)
    return attention, new_maps.reshape(2, H, E, E), new_moments


def solution(mesh):
    in_specs = (
        P(("groups", "seq"), None),
        P(("groups", "seq"), None),
        P(("groups", "seq"), None),
        P(("groups", "seq"), None),
        P(),
        P(),
        P("seq", None),
        P("seq", None),
    )
    out_specs = (
        P(("groups", "seq"), None),
        P("groups", None, None, None),
        P("groups", "seq", None),
    )
    return jax.shard_map(
        functools.partial(local, mesh.shape["seq"]),
        mesh=mesh, in_specs=in_specs, out_specs=out_specs, check_vma=False,
    )
```

```python
import functools

import jax
import jax.numpy as jnp
from jax import lax
from jax.experimental import pallas as pl
from jax.experimental.pallas import tpu as pltpu
from jax.sharding import PartitionSpec as P

H = 8
E = 128
SPAN = 256
OPT_STEP = 10
PAIRS = 4

BETA_ONE = 0.9
BETA_TWO = 0.95
RATE = 0.01
TINY = 1e-08
NORM_EPS = 1e-06

F32 = jnp.float32
BF16 = jnp.bfloat16


def dot(left, right, left_dim, right_dim):
    return lax.dot_general(
        left, right, (((left_dim,), (right_dim,)), ((), ())), preferred_element_type=F32
    )


def adam_rows(gradient, weights, first_old, second_old):
    first_new = BETA_ONE * first_old + (1.0 - BETA_ONE) * gradient
    second_new = BETA_TWO * second_old + (1.0 - BETA_TWO) * gradient * gradient
    first_hat = first_new / (1.0 - BETA_ONE**OPT_STEP)
    second_hat = second_new / (1.0 - BETA_TWO**OPT_STEP)
    return (weights - RATE * first_hat / (jnp.sqrt(second_hat) + TINY), first_new, second_new)


def layout(count):
    chips = count // 2
    row = 1
    while row * row * 4 <= chips:
        row *= 2
    return chips // row, row


def kernel(
    depth, width, share,
    queries_hbm, keys_hbm, values_hbm, out_grad_hbm, maps_hbm, first_hbm, second_hbm, gain,
    attention_hbm, new_maps, new_moments,
    queries, keys, values, out_grad, maps, first_old, second_old,
    gain_row, attention,
    feat_q, feat_k, slope_q, slope_k, raw_part, grad_raw, local_fk,
    states, core_in, chip, row_in, chain_in, chain_out, share_out, summed,
    grads, grads_core, grads_chip, grads_row, grads_part, rows_in,
    load, store,
    send_core, recv_core, send_row, recv_row, send_z, recv_z, send_share, recv_share,
    send_rc, recv_rc, send_ry, recv_ry, send_rz, recv_rz,
    send_gz, recv_gz, send_gy, recv_gy, send_gc, recv_gc,
):
    group = lax.axis_index("groups")
    me = lax.axis_index("seq")
    plane = 2 * width
    level = me // plane
    row = (me // 2) % width
    core = me % 2
    other_core = 1 - core
    half = depth // 2
    chunks = half * width
    per_pair = chunks // PAIRS
    rows_beside = [(row + step) % width for step in range(1, width)]
    levels = [(level + step) % depth for step in range(1, depth)]

    def index(to_level, to_row, to_core):
        return to_level * plane + to_row * 2 + to_core

    def remote(src, dst, send, recv, to_level, to_row, to_core):
        return pltpu.make_async_remote_copy(
            src_ref=src, dst_ref=dst, send_sem=send, recv_sem=recv,
            device_id=(group, index(to_level, to_row, to_core)),
            device_id_type=pl.DeviceIdType.MESH,
        )

    def span(start, size):
        return pl.ds(pl.multiple_of(start, size), size)

    def head_rows(head):
        return span(head * E, E)

    def greet(to):
        pl.semaphore_signal(
            barrier, inc=1, device_id=(group, to), device_id_type=pl.DeviceIdType.MESH
        )

    loads = [
        pltpu.make_async_copy(src, dst, load.at[slot])
        for slot, (src, dst) in enumerate(
            (
                (keys_hbm, keys),
                (maps_hbm, maps),
                (values_hbm, values),
                (queries_hbm, queries),
                (out_grad_hbm, out_grad),
                (first_hbm, first_old),
                (second_hbm, second_old),
            )
        )
    ]
    for one in loads:
        one.start()

    barrier = pltpu.get_barrier_semaphore()
    greet(index(level, row, other_core))
    for beside in rows_beside:
        greet(index(level, beside, core))
    for other in levels:
        greet(index(other, row, core))

    def masked(scores):
        line = lax.broadcasted_iota(jnp.int32, (SPAN, SPAN), 0)
        column = lax.broadcasted_iota(jnp.int32, (SPAN, SPAN), 1)
        return jnp.where(line >= column, scores, 0.0).astype(BF16)

    def both(body, pair):
        body(2 * pair)
        body(2 * pair + 1)

    def core_copy(way, pair):
        return remote(
            states.at[way, head_rows(2 * pair + other_core)], core_in.at[way, pair],
            send_core.at[way, pair], recv_core.at[way, pair], level, row, other_core,
        )

    def row_copy(way, pair, beside):
        return remote(
            chip.at[way, pair], row_in.at[way, row, pair],
            send_row.at[way, beside, pair], recv_row.at[way, row, pair], level, beside, core,
        )

    def row_arrival(way, pair, beside):
        return remote(
            chip.at[way, pair], row_in.at[way, beside, pair],
            send_row.at[way, row, pair], recv_row.at[way, beside, pair], level, beside, core,
        )

    def chain_copy(way, pair):
        return remote(
            chain_out.at[way, pair], chain_in.at[way, pair],
            send_z.at[way, pair], recv_z.at[way, pair],
            (level + (depth - 1 if way else 1)) % depth, row, core,
        )

    def share_copy(way, pair):
        mine = head_rows(2 * pair + core)
        return remote(
            share_out.at[way, pair], summed.at[way, mine],
            send_share.at[way, pair], recv_share.at[way, pair], level, row, other_core,
        )

    def share_arrival(way, pair):
        theirs = head_rows(2 * pair + other_core)
        return remote(
            share_out.at[way, pair], summed.at[way, theirs],
            send_share.at[way, pair], recv_share.at[way, pair], level, row, other_core,
        )

    def scan_rows(way, pair):
        core_copy(way, pair).wait_recv()
        own = states[way, head_rows(2 * pair + core), :]
        total = own + core_in[way, pair]
        chip[way, pair] = total
        for beside in rows_beside:
            row_copy(way, pair, beside).start()
        row_in[way, row, pair] = total

    def scan_levels(way, pair, first):
        last = 0 if way else depth - 1

        def steps():
            for beside in rows_beside:
                row_arrival(way, pair, beside).wait_recv()
            ahead = jnp.zeros((E, E), F32)
            total = jnp.zeros((E, E), F32)
            for member in range(width):
                one = row_in[way, member, pair]
                total = total + one
                counts = (member > row) if way else (member < row)
                ahead = ahead + jnp.where(counts, one, 0.0)
            if first:
                chain_out[way, pair] = total
                chain_copy(way, pair).start()
            else:
                chain_copy(way, pair).wait_recv()
                running = chain_in[way, pair]
                ahead = ahead + running

                @pl.when(level != last)
                def _():
                    chain_out[way, pair] = running + total
                    chain_copy(way, pair).start()

            near = core == (1 if way else 0)
            mine = head_rows(2 * pair + core)
            share_out[way, pair] = ahead + jnp.where(near, states[way, mine, :], 0.0)
            share_copy(way, pair).start()
            summed[way, mine, :] = ahead + jnp.where(near, 0.0, core_in[way, pair])

        at_first = level == (depth - 1 if way else 0)
        pl.when(at_first if first else jnp.logical_not(at_first))(steps)

    def scan_drain(way):
        last = 0 if way else depth - 1
        for pair in range(PAIRS):
            core_copy(way, pair).wait_send()
            share_copy(way, pair).wait_send()
            for beside in rows_beside:
                row_copy(way, pair, beside).wait_send()

            @pl.when(level != last)
            def _():
                chain_copy(way, pair).wait_send()

    def piece(chunk, of_core):
        return span((chunk * 2 + of_core) * share, share)

    def reduce_core_copy(side, chunk):
        return remote(
            grads.at[side, piece(chunk, other_core)], grads_core.at[side, chunk],
            send_rc.at[side, chunk], recv_rc.at[side, chunk], level, row, other_core,
        )

    def reduce_row_copy(side, chunk):
        which, to_row = chunk // width, chunk % width
        return remote(
            grads_chip.at[side, chunk], grads_row.at[side, which, row],
            send_ry.at[side, chunk], recv_ry.at[side, which, row], level, to_row, core,
        )

    def reduce_row_arrival(side, which, beside):
        return remote(
            grads_chip.at[side, 0], grads_row.at[side, which, beside],
            send_ry.at[side, 0], recv_ry.at[side, which, beside], level, beside, core,
        )

    def owner_copy(side, which):
        return remote(
            grads_part.at[side, which], rows_in.at[level],
            send_rz.at[side, which], recv_rz.at[level], side * half + which, row, core,
        )

    def owner_arrival(other):
        return remote(
            grads_part.at[0, 0], rows_in.at[other],
            send_rz.at[0, 0], recv_rz.at[other], other, row, core,
        )

    def reduce_start(side, pair):
        for chunk in range(pair * per_pair, (pair + 1) * per_pair):
            reduce_core_copy(side, chunk).start()

    def reduce_rows(side, pair):
        for chunk in range(pair * per_pair, (pair + 1) * per_pair):
            which, to_row = chunk // width, chunk % width
            reduce_core_copy(side, chunk).wait_recv()
            total = grads[side, piece(chunk, core), :] + grads_core[side, chunk]

            @pl.when(row == to_row)
            def _():
                grads_row[side, which, row] = total

            @pl.when(row != to_row)
            def _():
                grads_chip[side, chunk] = total
                reduce_row_copy(side, chunk).start()

    def reduce_levels(side, which):
        for beside in rows_beside:
            reduce_row_arrival(side, which, beside).wait_recv()
        total = grads_row[side, which, 0]
        for member in range(1, width):
            total = total + grads_row[side, which, member]

        @pl.when(level == side * half + which)
        def _():
            rows_in[level] = total

        @pl.when(level != side * half + which)
        def _():
            grads_part[side, which] = total
            owner_copy(side, which).start()

    def map_rows(of_level, of_row, of_core):
        return new_maps.at[span(index(of_level, of_row, of_core) * share, share)]

    def map_level_copy(side, other):
        mine = map_rows(level, row, core)
        return remote(
            mine, mine, send_gz.at[other], recv_gz.at[side, level - side * half],
            other, row, core,
        )

    def map_level_arrival(side, which):
        owner = side * half + which
        theirs = map_rows(owner, row, core)
        return remote(
            theirs, theirs, send_gz.at[owner], recv_gz.at[side, which], owner, row, core
        )

    def map_row_copy(side, which, beside):
        mine = map_rows(side * half + which, row, core)
        return remote(
            mine, mine, send_gy.at[side, which, beside], recv_gy.at[side, which, row],
            level, beside, core,
        )

    def map_row_arrival(side, which, beside):
        theirs = map_rows(side * half + which, beside, core)
        return remote(
            theirs, theirs, send_gy.at[side, which, row], recv_gy.at[side, which, beside],
            level, beside, core,
        )

    def map_core_copy(side, which, of_row):
        mine = map_rows(side * half + which, of_row, core)
        return remote(
            mine, mine, send_gc.at[side, which, of_row], recv_gc.at[side, which, of_row],
            level, row, other_core,
        )

    def map_core_arrival(side, which, of_row):
        theirs = map_rows(side * half + which, of_row, other_core)
        return remote(
            theirs, theirs, send_gc.at[side, which, of_row], recv_gc.at[side, which, of_row],
            level, row, other_core,
        )

    def update(side):
        @pl.when(level // half == side)
        def _():
            for other in levels:
                owner_arrival(other).wait_recv()
            gradient = rows_in[0]
            for other in range(1, depth):
                gradient = gradient + rows_in[other]
            mine = span(me * share, share)
            rows_new, first_new, second_new = adam_rows(
                gradient, maps[mine, :], first_old[...], second_old[...]
            )
            new_maps[mine, :] = rows_new
            if side == 0:
                for which in range(half):
                    owner_copy(1, which).wait_send()
            for other in levels:
                map_level_copy(side, other).start()
            own = level - side * half
            for beside in rows_beside:
                map_row_copy(side, own, beside).start()
            map_core_copy(side, own, row).start()
            new_moments[0] = first_new
            new_moments[1] = second_new

    def spread(side):
        for which in range(half):

            @pl.when(level != side * half + which)
            def _():
                map_level_arrival(side, which).wait_recv()
                for beside in rows_beside:
                    map_row_copy(side, which, beside).start()
                map_core_copy(side, which, row).start()

    def spread_core(side):
        for which in range(half):
            for beside in rows_beside:
                map_row_arrival(side, which, beside).wait_recv()
                map_core_copy(side, which, beside).start()

    def spread_queries():
        spread(0)
        spread_core(0)

    def spread_end(side):
        for which in range(half):
            for of_row in range(width):
                map_core_arrival(side, which, of_row).wait_recv()

    def drain(side):
        for chunk in range(chunks):
            reduce_core_copy(side, chunk).wait_send()

            @pl.when(row != chunk % width)
            def _():
                reduce_row_copy(side, chunk).wait_send()

        for which in range(half):
            for beside in rows_beside:
                map_row_copy(side, which, beside).wait_send()
            for of_row in range(width):
                map_core_copy(side, which, of_row).wait_send()

            passed = level != side * half + which
            if side == 1:
                passed = jnp.logical_and(passed, level >= half)

            @pl.when(passed)
            def _():
                owner_copy(side, which).wait_send()

        @pl.when(level // half == side)
        def _():
            for other in levels:
                map_level_copy(side, other).wait_send()

    def feature(source, weights, feat, slope, cols):
        pre = dot(source[:, cols], weights.astype(BF16), 1, 0)
        sigmoid = 0.5 + 0.5 * jnp.tanh(0.5 * pre)
        feat[:, cols] = (pre * sigmoid).astype(BF16)
        slope[:, cols] = sigmoid * (1.0 + pre * (1.0 - sigmoid))

    def key_features(head):
        cols = head_rows(head)
        feature(keys, maps[head_rows(H + head), :], feat_k, slope_k, cols)
        states[0, head_rows(head), :] = dot(feat_k[:, cols], values[:, cols], 0, 0)

    def query_features(head):
        cols = head_rows(head)
        feature(queries, maps[head_rows(head), :], feat_q, slope_q, cols)

    def inside(head):
        cols = head_rows(head)
        scores = masked(dot(feat_q[:, cols], feat_k[:, cols], 1, 1))
        raw_part[:, cols] = dot(scores, values[:, cols], 1, 0)

    def forward(head):
        cols = head_rows(head)
        before = summed[0, head_rows(head), :].astype(BF16)
        raw = dot(feat_q[:, cols], before, 1, 0) + raw_part[:, cols]
        scale = lax.rsqrt(jnp.mean(raw * raw, -1, keepdims=True) + NORM_EPS)
        unit = raw * scale
        wide = gain_row[:, cols]
        attention[:, cols] = (unit * wide).astype(BF16)
        dunit = out_grad[:, cols].astype(F32) * wide
        inner = jnp.mean(dunit * unit, -1, keepdims=True)
        grad = (scale * (dunit - unit * inner)).astype(BF16)
        grad_raw[:, cols] = grad
        states[1, head_rows(head), :] = dot(feat_q[:, cols], grad, 0, 0)

    def query_side(head):
        cols = head_rows(head)
        grad = grad_raw[:, cols]
        pscores = masked(dot(grad, values[:, cols], 1, 1))
        before = summed[0, head_rows(head), :].astype(BF16)
        grad_fq = dot(grad, before, 1, 1) + dot(pscores, feat_k[:, cols], 1, 0)
        local_fk[:, cols] = dot(pscores, feat_q[:, cols], 0, 0)
        grad_pq = (grad_fq * slope_q[:, cols]).astype(BF16)
        grads[0, head_rows(head), :] = dot(queries[:, cols], grad_pq, 0, 0)

    def key_side(head):
        cols = head_rows(head)
        after = summed[1, head_rows(head), :].astype(BF16)
        grad_fk = dot(values[:, cols], after, 1, 1) + local_fk[:, cols]
        grad_pk = (grad_fk * slope_k[:, cols]).astype(BF16)
        grads[1, head_rows(head), :] = dot(keys[:, cols], grad_pk, 0, 0)

    def keys_pair(pair):
        both(key_features, pair)
        if pair == 0:
            pl.semaphore_wait(barrier, 1 + width - 1 + depth - 1)
        core_copy(0, pair).start()

    def forward_pair(pair):
        share_arrival(0, pair).wait_recv()
        both(forward, pair)
        core_copy(1, pair).start()

    def query_pair(pair):
        both(query_side, pair)
        reduce_start(0, pair)

    def reduce_queries():
        for which in range(half):
            reduce_levels(0, which)

    def key_pair(pair):
        share_arrival(1, pair).wait_recv()
        both(key_side, pair)
        reduce_start(1, pair)

    for one in loads[:3]:
        one.wait()
    keys_pair(0)
    keys_pair(1)
    scan_rows(0, 0)
    keys_pair(2)
    scan_rows(0, 1)
    keys_pair(3)
    scan_rows(0, 2)
    for one in loads[3:]:
        one.wait()
    gain_row[...] = gain[...].astype(F32).reshape(1, H * E)
    both(query_features, 0)
    scan_rows(0, 3)
    both(query_features, 1)
    scan_levels(0, 0, True)
    both(query_features, 2)
    scan_levels(0, 1, True)
    both(query_features, 3)
    scan_levels(0, 2, True)
    both(inside, 0)
    scan_levels(0, 3, True)
    both(inside, 1)
    scan_levels(0, 0, False)
    both(inside, 2)
    scan_levels(0, 1, False)
    both(inside, 3)
    scan_levels(0, 2, False)
    forward_pair(0)
    scan_levels(0, 3, False)
    forward_pair(1)
    scan_rows(1, 0)
    forward_pair(2)
    scan_rows(1, 1)
    forward_pair(3)
    leave = pltpu.make_async_copy(attention, attention_hbm, store)
    leave.start()
    scan_rows(1, 2)
    scan_levels(1, 0, True)
    query_pair(0)
    scan_rows(1, 3)
    scan_levels(1, 1, True)
    query_pair(1)
    scan_levels(1, 2, True)
    query_pair(2)
    scan_levels(1, 3, True)
    query_pair(3)
    for pair in range(PAIRS):
        reduce_rows(0, pair)
    pl.when(level < half)(reduce_queries)
    scan_levels(1, 0, False)
    scan_levels(1, 1, False)
    scan_levels(1, 2, False)
    key_pair(0)
    scan_levels(1, 3, False)
    pl.when(level >= half)(reduce_queries)
    key_pair(1)
    reduce_rows(1, 0)
    key_pair(2)
    reduce_rows(1, 1)
    key_pair(3)
    reduce_rows(1, 2)
    reduce_rows(1, 3)
    for which in range(half):
        reduce_levels(1, which)
    update(0)
    update(1)
    pl.when(level < half)(spread_queries)
    spread(1)
    spread_core(1)
    pl.when(level >= half)(spread_queries)
    spread_end(0)
    spread_end(1)
    scan_drain(0)
    scan_drain(1)
    drain(0)
    drain(1)
    leave.wait()


def hand_over(sources, targets, staged, arrive, leave):
    moves = []
    for source, target, stage in zip(sources, targets, staged):
        rows = source.shape[0]
        size = min(rows, max(rows // 4, SPAN // 2))
        for start in range(0, rows, size):
            here = pl.ds(start, size)
            slot = len(moves)
            moves.append((
                pltpu.make_async_copy(source.at[here], stage.at[here], arrive.at[slot]),
                pltpu.make_async_copy(stage.at[here], target.at[here], leave.at[slot]),
            ))
    for into, _ in moves:
        into.start()
    for into, out in moves:
        into.wait()
        out.start()
    for _, out in moves:
        out.wait()


def local(count, queries, keys, values, out_grad, maps, gain, first_moment, second_moment):
    depth, width = layout(count)
    half = depth // 2
    share = 2 * H * E // count
    tokens = queries.shape[0]
    wide = (SPAN, H * E)
    flat = (2 * H * E, E)
    square = (2, PAIRS, E, E)
    dma = pltpu.SemaphoreType.DMA
    chunks = half * width
    scratch = [
        pltpu.VMEM(wide, BF16),
        pltpu.VMEM(wide, BF16),
        pltpu.VMEM(wide, BF16),
        pltpu.VMEM(wide, BF16),
        pltpu.VMEM(flat, F32),
        pltpu.VMEM((share, E), F32),
        pltpu.VMEM((share, E), F32),
        pltpu.VMEM((1, H * E), F32),
        pltpu.VMEM(wide, BF16),
        pltpu.VMEM(wide, BF16),
        pltpu.VMEM(wide, BF16),
        pltpu.VMEM(wide, F32),
        pltpu.VMEM(wide, F32),
        pltpu.VMEM(wide, F32),
        pltpu.VMEM(wide, BF16),
        pltpu.VMEM(wide, F32),
        pltpu.VMEM((2, H * E, E), F32),
        pltpu.VMEM(square, F32),
        pltpu.VMEM(square, F32),
        pltpu.VMEM((2, width, PAIRS, E, E), F32),
        pltpu.VMEM(square, F32),
        pltpu.VMEM(square, F32),
        pltpu.VMEM(square, F32),
        pltpu.VMEM((2, H * E, E), F32),
        pltpu.VMEM((2, H * E, E), F32),
        pltpu.VMEM((2, chunks, share, E), F32),
        pltpu.VMEM((2, chunks, share, E), F32),
        pltpu.VMEM((2, half, width, share, E), F32),
        pltpu.VMEM((2, half, share, E), F32),
        pltpu.VMEM((depth, share, E), F32),
        dma((7,)),
        dma,
        dma((2, PAIRS)),
        dma((2, PAIRS)),
        dma((2, width, PAIRS)),
        dma((2, width, PAIRS)),
        dma((2, PAIRS)),
        dma((2, PAIRS)),
        dma((2, PAIRS)),
        dma((2, PAIRS)),
        dma((2, chunks)),
        dma((2, chunks)),
        dma((2, chunks)),
        dma((2, half, width)),
        dma((2, half)),
        dma((depth,)),
        dma((depth,)),
        dma((2, half)),
        dma((2, half, width)),
        dma((2, half, width)),
        dma((2, half, width)),
        dma((2, half, width)),
    ]
    vmem = pl.BlockSpec(memory_space=pltpu.VMEM)
    anywhere = pl.BlockSpec(memory_space=pl.ANY)
    attention, new_maps, new_moments = pl.pallas_call(
        functools.partial(kernel, depth, width, share),
        out_shape=(
            jax.ShapeDtypeStruct((tokens, H * E), BF16),
            jax.ShapeDtypeStruct(flat, F32),
            jax.ShapeDtypeStruct((2, share, E), F32),
        ),
        in_specs=[anywhere] * 7 + [vmem],
        out_specs=(anywhere, vmem, vmem),
        scratch_shapes=scratch,
        compiler_params=pltpu.CompilerParams(
            collective_id=0, has_side_effects=True, vmem_limit_bytes=60 * 1024 * 1024
        ),
        name="layer",
    )(
        queries, keys, values, out_grad, maps.reshape(flat),
        first_moment, second_moment, gain,
    )
    results = (attention, new_maps, new_moments)
    attention, new_maps, new_moments = pl.pallas_call(
        lambda *refs: hand_over(refs[:3], refs[3:6], refs[6:9], *refs[9:]),
        out_shape=tuple(jax.ShapeDtypeStruct(one.shape, one.dtype) for one in results),
        in_specs=[anywhere] * 3,
        out_specs=(anywhere,) * 3,
        scratch_shapes=[pltpu.VMEM(one.shape, one.dtype) for one in results]
        + [dma((8,)), dma((8,))],
        compiler_params=pltpu.CompilerParams(vmem_limit_bytes=63 * 1024 * 1024),
        name="results",
    )(*results)
    return attention, new_maps.reshape(2, H, E, E), new_moments


def solution(mesh):
    in_specs = (
        P(("groups", "seq"), None),
        P(("groups", "seq"), None),
        P(("groups", "seq"), None),
        P(("groups", "seq"), None),
        P(),
        P(),
        P("seq", None),
        P("seq", None),
    )
    out_specs = (
        P(("groups", "seq"), None),
        P("groups", None, None, None),
        P("groups", "seq", None),
    )
    return jax.shard_map(
        functools.partial(local, mesh.shape["seq"]),
        mesh=mesh, in_specs=in_specs, out_specs=out_specs, check_vma=False,
    )
```
